32 devices in a mesh: stream: 2 (over y), span: 4 (over z), vert: 4 (over x, core).
Axes of the slice: x: 2, y: 2, z: 4, core: 2. Of those that a mesh axis runs over, the one named last changes fastest.
Arguments:
- fields: float32 [5, 128, 64, 256], P(None, 'vert', 'span', 'stream'), may hold values from -6 to 6
- solid_frac: float32 [128, 64, 256], P('vert', 'span', 'stream'), may hold values from 0 to 1
- panels: float32 [512, 5, 256], P(('stream', 'span', 'vert')), may hold values from -0.0625 to 0.0625
- panel_owner: int32 [512, 1], P(('stream', 'span', 'vert')), may hold values from 0 to 15; in each aligned block of 16 rows (0 to 15, 16 to 31, ...) at most 2 rows name the same one
- deck_cells: int32 [4, 4, 2, 2048], P('vert', 'span', 'stream'), may hold values from 0 to 65535
- deck_geom: float32 [4, 4, 2, 3, 2048], P('vert', None, 'stream'), may hold values from -6 to 6
- strip_ids: int32 [4, 4, 2, 2048], P('vert', None, 'stream'), may hold values from 0 to 15, as said below
- mode_shapes: float32 [3, 16, 32], replicated, may hold values from -0.013671875 to 0.013671875
Outputs:
- new_fields: float32 [5, 128, 64, 256], P(None, 'vert', 'span', 'stream')
- modal_force: float32 [32], replicated
The draws below stay inside these ranges and needn't reach their ends.
Inputs may be any that keep to these rules, and one draw needn't show every extreme that they name: `panel_owner`: tile number s * 4 + v for along-deck tile s and vertical tile v. Among the 16 panels of one device no tile is named more than 2 times; some device names some tile exactly 2 times. `strip_ids`: cells of along-deck tile s belong to strips s * 4 to (s + 1) * 4 - 1.
All inputs are finite; a program needn't handle non-finite values.
Results may differ from the reference program's by a relative error of at most 0.00012.
Values sent between devices are 32-bit elements; how exact they have to be, the bound alone decides.
A program may use at most 128 MiB of HBM per device.

```python
import math
import jax
import jax.numpy as jnp
import numpy as np
from jax import lax

CX = 128
CY = 16
CZ = 32
SPEC = 128
CAP = 2
DECK_DEV = 2048
STRIP_DEV = 4
MODES = 32
NX = 256
NY = 64
NZ = 128
PAN_DEV = 16
PANELS = 512
NSTRIP = 16
N_STREAM = 2
N_SPAN = 4
N_VERT = 4
DEVICES = 32


def draw_strip_ids(key, part):
    offsets = jax.random.randint(key, (N_VERT, N_SPAN, N_STREAM, DECK_DEV), 0, STRIP_DEV, dtype=jnp.int32)
    starts = (jnp.arange(N_SPAN, dtype=jnp.int32) * STRIP_DEV)[None, :, None, None]
    return (starts + offsets).astype(jnp.int32)


def touch_ends(values, own_key, low, high):
    longest = values.shape.index(max(values.shape))
    spots = []
    for shift in (0, 1):
        where = [jax.random.randint(jax.random.fold_in(own_key, axis), (), 0, length) for axis, length in enumerate(values.shape)]
        where[longest] = (where[longest] + shift) % values.shape[longest]
        spots.append(tuple(where))
    return values.at[spots[0]].set(low).at[spots[1]].set(high)


def levels(stream_key, extent, split, low, largest):
    level, own = 1.0, jax.random.fold_in(stream_key, 6)
    for position, parts in split:
        draws = jnp.exp(jax.random.uniform(jax.random.fold_in(own, position), (parts,), jnp.float32, low / len(split), largest / len(split)))
        level = level * jnp.repeat(draws, extent[position] // parts).reshape([-1 if axis == position else 1 for axis in range(len(extent))])
    return level


def routed_block(rng, own, number, rows, amount, top, bound, slope):
    sequence = jax.random.permutation(rng, amount)
    heavy_load, ordinary = load_shares(amount, rows * top, bound, slope, True), load_shares(amount, rows * top, bound, slope, False)
    places = jnp.arange(amount)

    def named(tallies, turn):
        used = int((tallies > 0).sum())
        fixed = max(1, used // 4)
        passed = fixed + (places - fixed + turn * (used - fixed)) % max(1, amount - fixed)
        return jnp.zeros((amount,), jnp.int32).at[sequence[jnp.where(places < fixed, places, passed)]].set(jnp.asarray(tallies, jnp.int32))

    tallies = jnp.where(number % 4 == 0, named(heavy_load, number // 4), named(ordinary, number - number // 4 - 1))
    mixed = jax.random.permutation(jax.random.fold_in(own, 3), amount)
    source_of, sink = mixed[0:amount // 2 * 2:2], mixed[1:amount // 2 * 2:2]
    slack = jnp.minimum(tallies[source_of] - 1, bound - tallies[sink]) // 2
    slack = jnp.where((source_of == sequence[0]) | (sink == sequence[0]) | (tallies[sink] == 0), 0, jnp.maximum(slack, 0))
    passed = jax.random.randint(jax.random.fold_in(own, 4), (amount // 2,), 0, 1 << 20) % (slack + 1)
    tallies = tallies.at[source_of].add(-passed).at[sink].add(passed)
    labels = jnp.searchsorted(jnp.cumsum(tallies), jnp.arange(rows * top), side="right").astype(jnp.int32)
    table = labels.reshape(top, rows).T
    table = table[jax.random.permutation(jax.random.fold_in(own, 1), rows)]
    turn = jax.random.randint(jax.random.fold_in(own, 2), (rows, 1), 0, top)
    return jnp.take_along_axis(table, (jnp.arange(top)[None, :] + turn) % top, axis=1)


def load_shares(count, total, reach, lean, full):
    weights = [(1 << 20) // math.isqrt(rank ** lean) + 1 for rank in range(1, count + 1)]
    largest = reach if full else min(reach, max(-(-total // count), total * weights[0] // sum(weights)))
    least = 1 if total - largest >= count - 1 else 0
    given, surplus = [largest] + [least] * (count - 1), total - largest - least * (count - 1)
    while surplus > 0:
        candidates = [i for i in range(1, count) if given[i] < largest] or [i for i in range(1, count) if given[i] < reach]
        mass, left = sum([weights[i] for i in candidates]), surplus
        for i in candidates:
            extra = min(reach - given[i], max(1, left * weights[i] // mass), surplus)
            given[i] = given[i] + extra
            surplus = surplus - extra
    return np.array(given)


def scatter_about(own_key, shape, scale, bound, cuts=(), kind=jnp.bfloat16):
    drawn = jax.random.normal(own_key, shape, jnp.float32) * scale
    if len(cuts) > 0:
        drawn = levels(own_key, shape, cuts, -0.22, 0.18) * drawn
    return jnp.clip(drawn, min=-bound, max=bound).astype(kind)


def setup_inputs(seed: int = 0) -> dict:
    seeds = jax.random.split(jax.random.key(seed), 9)
    fields = scatter_about(seeds[0], (5, NZ, NY, NX), 1.0, 6.0, ((1, 4), (2, 4), (3, 2)), jnp.float32)
    solid_frac = jnp.clip(1.0 * jax.random.uniform(seeds[1], (NZ, NY, NX), jnp.float32) ** levels(seeds[1], (NZ, NY, NX), ((0, 4), (1, 4), (2, 2)), -0.2, 0.2), 0.0, 1.0)
    panels = scatter_about(seeds[2], (PANELS, 5, 2 * SPEC), (2 * SPEC * PAN_DEV * N_STREAM) ** -0.5, 0.0625, ((0, 32),), jnp.float32)
    panel_owner_keys = jax.random.split(jax.random.fold_in(seeds[3], 1), PANELS // PAN_DEV)
    panel_owner_turns = jax.random.permutation(jax.random.fold_in(seeds[3], 3), PANELS // PAN_DEV)
    panel_owner = jax.vmap(lambda own, number: routed_block(jax.random.fold_in(seeds[3], 2), own, number, PAN_DEV, N_SPAN * N_VERT, 1, CAP, 2))(panel_owner_keys, panel_owner_turns).reshape((PANELS, 1))
    deck_cells = touch_ends(jax.random.randint(seeds[4], (N_VERT, N_SPAN, N_STREAM, DECK_DEV), 0, CX * CY * CZ), jax.random.fold_in(seeds[4], 1), 0, (CX * CY * CZ) - 1).astype(jnp.int32)
    deck_geom = scatter_about(seeds[5], (N_VERT, N_SPAN, N_STREAM, 3, DECK_DEV), 1.0, 6.0, ((0, 4), (2, 2)), jnp.float32)
    strip_ids = draw_strip_ids(jax.random.fold_in(seeds[8], 71), 0)
    mode_shapes = scatter_about(seeds[7], (3, NSTRIP, MODES), (3 * DECK_DEV * DEVICES) ** -0.5, 0.013671875, (), jnp.float32)
    return dict(fields=fields, solid_frac=solid_frac, panels=panels, panel_owner=panel_owner, deck_cells=deck_cells, deck_geom=deck_geom, strip_ids=strip_ids, mode_shapes=mode_shapes)


time_step = 0.15
viscous = 0.05
heat_diff = 0.03
sound_sq = 1.0
buoyant = 0.5
penalty = 0.5
relax_time = 0.5
relax_depth = 8.0
wave_cols = 16


def wave_basis(heights, widths, total_z, total_y, spec):
    modes = jnp.arange(spec, dtype=jnp.int32)
    across = (modes % wave_cols)[:, None, None]
    upward = (modes // wave_cols)[:, None, None]
    period = total_y * total_z
    phase = (across * widths[None, None, :] * total_z + upward * heights[None, :, None] * total_y) % period
    angle = phase.astype(jnp.float32) * (2.0 * math.pi / period)
    return jnp.concatenate([jnp.cos(angle), jnp.sin(angle)], axis=0)


def relax_weights(positions, limit):
    spots = positions.astype(jnp.float32)
    return jnp.where(positions < limit, jnp.exp(-spots / relax_depth) / relax_time, 0.0)


def rates(padded, solid_frac, relax_rate, target_plane):
    centre = padded[:, 1:-1, 1:-1, 1:-1]
    east_side = padded[:, 1:-1, 1:-1, 2:]
    west_side = padded[:, 1:-1, 1:-1, :-2]
    north_side = padded[:, 1:-1, 2:, 1:-1]
    south_side = padded[:, 1:-1, :-2, 1:-1]
    upper_side = padded[:, 2:, 1:-1, 1:-1]
    lower_side = padded[:, :-2, 1:-1, 1:-1]
    grad_x = 0.5 * (east_side - west_side)
    grad_y = 0.5 * (north_side - south_side)
    grad_z = 0.5 * (upper_side - lower_side)
    laplace = east_side + west_side + north_side + south_side + upper_side + lower_side - 6.0 * centre
    speed_x = centre[0]
    speed_y = centre[1]
    speed_z = centre[2]
    carried = speed_x * grad_x + speed_y * grad_y + speed_z * grad_z
    coeffs = jnp.array([viscous, viscous, viscous, viscous, heat_diff], jnp.float32)[:, None, None, None]
    damping = solid_frac / penalty
    nudging = relax_rate[None, None, None, :] * (target_plane[:, :, :, None] - centre)
    common = coeffs * laplace - carried + nudging
    extra_terms = jnp.stack([
        -grad_x[3] - damping * speed_x,
        -grad_y[3] - damping * speed_y,
        -grad_z[3] - damping * speed_z + buoyant * centre[4],
        -sound_sq * (grad_x[0] + grad_y[1] + grad_z[2]),
        jnp.zeros_like(speed_x)])
    return common + extra_terms


def reference(fields, solid_frac, panels, panel_owner, deck_cells, deck_geom, strip_ids, mode_shapes):
    tile_count = N_SPAN * N_VERT
    coeffs = jax.ops.segment_sum(panels.reshape(panels.shape[0], -1), panel_owner[:, 0], num_segments=tile_count)
    coeffs = coeffs.reshape(N_SPAN, N_VERT, 5, 2 * SPEC)
    wave_table = wave_basis(jnp.arange(NZ, dtype=jnp.int32), jnp.arange(NY, dtype=jnp.int32), NZ, NY, SPEC)
    wave_table = wave_table.reshape(2 * SPEC, N_VERT, CZ, N_SPAN, CY)
    inflow_plane = jnp.einsum('svfk,kvisj->fvisj', coeffs, wave_table, precision=lax.Precision.HIGHEST)
    inflow_plane = inflow_plane.reshape(5, NZ, NY)
    target_plane = inflow_plane + jnp.array([1.0, 0.0, 0.0, 0.0, 0.0], jnp.float32)[:, None, None]
    relax_rate = relax_weights(jnp.arange(NX, dtype=jnp.int32), CX // 2)

    def advance(state):
        padded = jnp.pad(state, ((0, 0), (1, 1), (1, 1), (1, 1)))
        return rates(padded, solid_frac, relax_rate, target_plane)

    first_update = fields + time_step * advance(fields)
    new_fields = 0.5 * (fields + first_update + time_step * advance(first_update))

    pressure = new_fields[3].reshape(N_VERT, CZ, N_SPAN, CY, N_STREAM, CX)
    pressure = pressure.transpose(0, 2, 4, 1, 3, 5).reshape(N_VERT, N_SPAN, N_STREAM, CZ * CY * CX)
    sampled = jnp.take_along_axis(pressure, deck_cells, axis=3)
    traction = sampled[:, :, :, None, :] * deck_geom
    traction = traction.transpose(3, 0, 1, 2, 4).reshape(3, -1)
    forces = jax.ops.segment_sum(traction.T, strip_ids.reshape(-1), num_segments=NSTRIP)
    modal_force = jnp.einsum('jc,cjm->m', forces, mode_shapes, precision=lax.Precision.HIGHEST)
    return new_fields, modal_force
```

```python
import functools
import math

import jax
import jax.numpy as jnp
from jax import lax
from jax.experimental import pallas as pl
from jax.experimental.pallas import tpu as pltpu
from jax.sharding import PartitionSpec as P

MESH = pl.DeviceIdType.MESH
HIGHEST = lax.Precision.HIGHEST

time_step = 0.15
viscous = 0.05
heat_diff = 0.03
sound_sq = 1.0
buoyant = 0.5
penalty = 0.5
relax_time = 0.5
relax_depth = 8.0
wave_cols = 16
FIELDS = 5
ROWS = 8
PARTS = 2


def split_index(values, size):
    if size & (size - 1) == 0:
        return values >> (size.bit_length() - 1), values & (size - 1)
    whole = lax.div(values, jnp.int32(size))
    return whole, values - whole * size


def circle(turns):
    quarter = jnp.floor(4.0 * turns + 0.5)
    angle = (turns - 0.25 * quarter) * (2.0 * math.pi)
    sq = angle * angle
    sine = angle * (
        1.0 + sq * (-1.0 / 6 + sq * (1.0 / 120 + sq * (-1.0 / 5040 + sq * (1.0 / 362880))))
    )
    cosine = 1.0 + sq * (
        -0.5 + sq * (1.0 / 24 + sq * (-1.0 / 720 + sq * (1.0 / 40320 + sq * (-1.0 / 3628800))))
    )
    odd = (quarter == 1.0) | (quarter == 3.0)
    cos_flip = jnp.where((quarter == 1.0) | (quarter == 2.0), -1.0, 1.0)
    sin_flip = jnp.where((quarter == 2.0) | (quarter == 3.0), -1.0, 1.0)
    return cos_flip * jnp.where(odd, sine, cosine), sin_flip * jnp.where(odd, cosine, sine)


def kernel(
    sizes,
    fields_ref,
    solid_ref,
    panels_ref,
    owner_ref,
    cells_ref,
    geom_ref,
    strips_ref,
    modes_ref,
    out_ref,
    modal_ref,
    state,
    update,
    result,
    x_send,
    x_recv,
    x_both,
    y_send,
    y_recv,
    pan_in,
    pan_send,
    pan_recv,
    co_send,
    co_recv,
    wave,
    target,
    press,
    md_send,
    md_recv,
    sd_send,
    sd_recv,
    local_sem,
    halo_s,
    halo_r,
    pan_s,
    pan_r,
    co_s,
    co_r,
    md_s,
    md_r,
    sd_s,
    sd_r,
):
    n_stream, n_span, n_vert = sizes
    tiles = n_span * n_vert
    depth, span_cells, wind = fields_ref.shape[1:]
    half = depth // PARTS
    per_group = min(FIELDS, (wind // 2) // half)
    groups = -(-FIELDS // per_group)
    held = panels_ref.shape[0]
    spec_cols = panels_ref.shape[2]
    spec = spec_cols // 2
    strip_share = modes_ref.shape[1] // n_span
    n_modes = modes_ref.shape[2]
    deck = cells_ref.shape[3]
    me = (lax.axis_index("stream"), lax.axis_index("span"), lax.axis_index("vert"))
    stream_pos, span_pos, vert_pos = me
    my_tile = span_pos * n_vert + vert_pos

    def tile_peer(step):
        peer = lax.rem(my_tile + step, tiles)
        whole = lax.div(peer, jnp.int32(n_vert))
        return peer, (stream_pos, whole, peer - whole * n_vert)

    def stream_peer(step):
        peer = lax.rem(stream_pos + step, n_stream)
        return peer, (peer, span_pos, vert_pos)

    load = pltpu.make_async_copy(fields_ref, state.at[:, pl.ds(1, depth)], local_sem.at[0])
    load.start()

    barrier = pltpu.get_barrier_semaphore()
    for step in range(1, tiles):
        pl.semaphore_signal(barrier, inc=1, device_id=tile_peer(step)[1], device_id_type=MESH)
    for step in range(1, n_stream):
        pl.semaphore_signal(barrier, inc=1, device_id=stream_peer(step)[1], device_id_type=MESH)

    pan_in[...] = jnp.zeros_like(pan_in)
    pan_in[:, 0:FIELDS, :] = panels_ref[...]
    owner = jnp.broadcast_to(owner_ref[...], (held, tiles * ROWS))
    owner = jnp.broadcast_to(owner[:, None, :], (held, ROWS, tiles * ROWS))
    owner = owner.reshape(held * ROWS, tiles * ROWS)
    row_field = lax.broadcasted_iota(jnp.int32, owner.shape, 0) & (ROWS - 1)
    col_tile, col_field = split_index(lax.broadcasted_iota(jnp.int32, owner.shape, 1), ROWS)
    route = jnp.where((owner == col_tile) & (row_field == col_field), 1.0, 0.0)
    sums = lax.dot_general(
        route,
        pan_in[...].reshape(held * ROWS, spec_cols),
        (((0,), (0,)), ((), ())),
        precision=HIGHEST,
        preferred_element_type=jnp.float32,
    )
    pan_send[...] = sums.reshape(tiles, ROWS, spec_cols)

    def halo(axis, way, src, dst, sem):
        count, place = sizes[axis], me[axis]
        up = way == 0
        to = lax.rem(place + (1 if up else count - 1), count)
        device = tuple(to if a == axis else me[a] for a in range(3))
        sends = place < count - 1 if up else place > 0
        gets = place > 0 if up else place < count - 1

        def copy():
            return pltpu.make_async_remote_copy(
                src_ref=src,
                dst_ref=dst,
                send_sem=halo_s.at[sem],
                recv_sem=halo_r.at[sem],
                device_id=device,
                device_id_type=MESH,
            )

        def start():
            pl.when(sends)(lambda: copy().start())

        def arrive():
            pl.when(gets)(lambda: copy().wait_recv())

        def leave():
            pl.when(sends)(lambda: copy().wait_send())

        def clear():
            @pl.when(jnp.logical_not(gets))
            def _():
                dst[...] = jnp.zeros(dst.shape, jnp.float32)

        return start, arrive, leave, clear

    z_first = [
        halo(2, 0, fields_ref.at[:, depth - 1], state.at[:, 0], 0),
        halo(2, 1, fields_ref.at[:, 0], state.at[:, depth + 1], 1),
    ]
    z_second = [
        halo(2, 0, update.at[:, depth], update.at[:, 0], 2),
        halo(2, 1, update.at[:, 1], update.at[:, depth + 1], 3),
    ]
    xy_first = [
        halo(1, way, y_send.at[0, way], y_recv.at[0, way], 4 + way) for way in range(2)
    ] + [halo(0, way, x_send.at[0], x_recv.at[0, way], 6 + way) for way in range(2)]
    xy_second = [
        [
            halo(1, way, y_send.at[1, way, part], y_recv.at[1, way, part], 8 + 4 * part + way)
            for way in range(2)
        ]
        + [
            halo(0, way, x_send.at[1, part], x_recv.at[1, way, part], 10 + 4 * part + way)
            for way in range(2)
        ]
        for part in range(PARTS)
    ]
    every_halo = z_first + z_second + xy_first + xy_second[0] + xy_second[1]

    lane = lax.broadcasted_iota(jnp.int32, (span_cells, wind), 1)
    row = lax.broadcasted_iota(jnp.int32, (span_cells, wind), 0)
    lane_pair = lane >> 1

    def pack(stage, part, z, values, held_x):
        packed = list(held_x)
        for f in range(FIELDS):
            y_send[stage, 0, part, f, pl.ds(z, 1), :] = values[f][span_cells - 1 : span_cells, :]
            y_send[stage, 1, part, f, pl.ds(z, 1), :] = values[f][0:1, :]
            pair = (f % per_group) * half + z
            turned = pltpu.roll(values[f], 2 * pair + 1, 1)
            g = f // per_group
            packed[g] = jnp.where(lane_pair == pair, turned, packed[g])
        return tuple(packed)

    no_columns = tuple(jnp.zeros((span_cells, wind), jnp.float32) for _ in range(groups))

    load.wait()
    for part in range(PARTS):

        def pack_plane(z, held_x, part=part):
            values = [state[f, 1 + part * half + z] for f in range(FIELDS)]
            return pack(0, part, z, values, held_x)

        packed = lax.fori_loop(0, half, pack_plane, no_columns)
        for g in range(groups):
            x_send[0, part, g] = packed[g]

    pl.semaphore_wait(barrier, tiles - 1 + n_stream - 1)

    def spread(peers, count, src, dst, mine, send_sem, recv_sem):
        copies = []
        for step in range(1, count):
            peer, device = peers(step)
            copy = pltpu.make_async_remote_copy(
                src_ref=src(peer),
                dst_ref=dst.at[mine],
                send_sem=send_sem.at[peer],
                recv_sem=recv_sem.at[mine],
                device_id=device,
                device_id_type=MESH,
            )
            copy.start()
            arrival = pltpu.make_async_remote_copy(
                src_ref=src(peer),
                dst_ref=dst.at[peer],
                send_sem=send_sem.at[peer],
                recv_sem=recv_sem.at[peer],
                device_id=device,
                device_id_type=MESH,
            )
            copies.append((copy, arrival))
        return copies

    pan_copies = spread(
        tile_peer, tiles, lambda peer: pan_send.at[peer], pan_recv, my_tile, pan_s, pan_r
    )
    for start, _, _, clear in z_first + xy_first:
        start()
    for _, _, _, clear in every_halo:
        clear()
    pan_recv[my_tile] = pan_send[my_tile]

    total_z, total_y = depth * n_vert, span_cells * n_span
    period = total_y * total_z
    plane = depth * span_cells
    cell_z, cell_y = split_index(lax.broadcasted_iota(jnp.int32, (plane, spec), 0), span_cells)
    upward, across = split_index(lax.broadcasted_iota(jnp.int32, (plane, spec), 1), wave_cols)
    phase = across * (span_pos * span_cells + cell_y) * total_z
    phase = phase + upward * (vert_pos * depth + cell_z) * total_y
    phase = split_index(phase, period)[1]
    cosine, sine = circle(phase.astype(jnp.float32) * (1.0 / period))
    wave[:, 0:spec] = cosine
    wave[:, spec:] = sine

    for _, arrival in pan_copies:
        arrival.wait_recv()
    mine = pan_recv[0]
    for t in range(1, tiles):
        mine = mine + pan_recv[t]
    co_send[...] = mine
    co_copies = spread(
        stream_peer, n_stream, lambda peer: co_send, co_recv, stream_pos, co_s, co_r
    )
    co_recv[stream_pos] = mine

    for _, arrive, _, _ in z_first + xy_first:
        arrive()
    even = (lane & 1) == 0

    def columns(stage, part):
        for g in range(groups):
            from_low = pltpu.roll(x_recv[stage, 0, part, g], 1, 1)
            from_high = pltpu.roll(x_recv[stage, 1, part, g], wind - 1, 1)
            x_both[stage, part, g] = jnp.where(even, from_high, from_low)

    for part in range(PARTS):
        columns(0, part)

    for _, arrival in co_copies:
        arrival.wait_recv()
    coeffs = co_recv[0]
    for t in range(1, n_stream):
        coeffs = coeffs + co_recv[t]
    inflow = lax.dot_general(
        wave[...],
        coeffs,
        (((1,), (1,)), ((), ())),
        precision=HIGHEST,
        preferred_element_type=jnp.float32,
    )
    first_field = lax.broadcasted_iota(jnp.int32, inflow.shape, 1) == 0
    target[...] = inflow + jnp.where(first_field, 1.0, 0.0)

    spots = stream_pos * wind + lane
    relax = jnp.where(
        spots < wind // 2, jnp.exp(spots.astype(jnp.float32) * (-1.0 / relax_depth)) / relax_time, 0.0
    )
    relax_dt = time_step * relax
    diffusion = [viscous] * 4 + [heat_diff]
    keep = {nu: 1.0 - time_step * (6.0 * nu) - relax_dt for nu in set(diffusion)}
    half_dt = 0.5 * time_step

    def advance(source, stage, part, z):
        at = part * half + z
        wanted = target[pl.ds(pl.multiple_of(at * span_cells, span_cells), span_cells), :]
        centre = [source[f, 1 + at] for f in range(FIELDS)]
        u, v, w = (half_dt * centre[f] for f in range(3))
        diff_x, diff_y, diff_z, new = [], [], [], []
        for f in range(FIELDS):
            c = centre[f]
            pair = (f % per_group) * half + z
            side = pltpu.roll(x_both[stage, part, f // per_group], wind - 1 - 2 * pair, 1)
            west = jnp.where(lane == 0, side, pltpu.roll(c, 1, 1))
            east = jnp.where(lane == wind - 1, side, pltpu.roll(c, wind - 1, 1))
            low = jnp.broadcast_to(y_recv[stage, 0, part, f, pl.ds(z, 1), :], c.shape)
            high = jnp.broadcast_to(y_recv[stage, 1, part, f, pl.ds(z, 1), :], c.shape)
            south = jnp.where(row == 0, low, pltpu.roll(c, 1, 0))
            north = jnp.where(row == span_cells - 1, high, pltpu.roll(c, span_cells - 1, 0))
            lower = source[f, at]
            upper = source[f, at + 2]
            dx, dy, dz = east - west, north - south, upper - lower
            around = (east + west) + (north + south) + (upper + lower)
            nu = diffusion[f]
            value = keep[nu] * c + (time_step * nu) * around
            value = value + relax_dt * jnp.broadcast_to(wanted[:, f : f + 1], c.shape)
            value = value - (u * dx + v * dy + w * dz)
            diff_x.append(dx)
            diff_y.append(dy)
            diff_z.append(dz)
            new.append(value)
        damping = (2.0 / penalty) * solid_ref[at]
        new[0] = new[0] - half_dt * diff_x[3] - damping * u
        new[1] = new[1] - half_dt * diff_y[3] - damping * v
        new[2] = new[2] - half_dt * diff_z[3] - damping * w + (time_step * buoyant) * centre[4]
        new[3] = new[3] - (half_dt * sound_sq) * (diff_x[0] + diff_y[1] + diff_z[2])
        return new

    for part in range(PARTS):

        def first_plane(z, held_x, part=part):
            new = advance(state, 0, part, z)
            for f in range(FIELDS):
                update[f, 1 + part * half + z] = new[f]
            return pack(1, part, z, new, held_x)

        packed = lax.fori_loop(0, half, first_plane, no_columns)
        for g in range(groups):
            x_send[1, part, g] = packed[g]
        for start, _, _, _ in xy_second[part]:
            start()
        if part == 0:
            z_second[1][0]()
    z_second[0][0]()

    def second_plane(part, z):
        new = advance(update, 1, part, z)
        at = part * half + z
        for f in range(FIELDS):
            value = 0.5 * (state[f, 1 + at] + new[f])
            result[f, at] = value
            if f == 3:
                top = value.astype(jnp.bfloat16)
                rest = (value - top.astype(jnp.float32)).astype(jnp.bfloat16)
                where = pl.ds(pl.multiple_of(at * span_cells, span_cells), span_cells)
                press[where, 0:wind] = top
                press[where, wind:] = rest

    def store(part):
        where = pl.ds(part * half, half)
        return pltpu.make_async_copy(
            result.at[:, where], out_ref.at[:, where], local_sem.at[1 + part]
        )

    for part in range(PARTS):
        for _, arrive, _, _ in xy_second[part]:
            arrive()
        columns(1, part)
        if part == PARTS - 1:
            z_second[1][1]()

        def plane_step(z, carry, part=part):
            second_plane(part, z)
            return carry

        lax.fori_loop(1 if part == 0 else 0, half, plane_step, 0)
        if part == 0:
            z_second[0][1]()
            second_plane(0, 0)
        store(part).start()

    width = min(deck, 256)
    base = span_pos * strip_share
    hit_row = lax.broadcasted_iota(jnp.int32, (plane, width), 0)
    hit_col = lax.broadcasted_iota(jnp.int32, (wind, width), 0)

    def deck_step(i, totals):
        where = pl.ds(pl.multiple_of(i * width, width), width)
        cell_row, cell_col = split_index(cells_ref[0, 0, :, where], wind)
        pick = jnp.where(hit_col == cell_col, 1.0, 0.0).astype(jnp.bfloat16)
        pick = jnp.concatenate([pick, pick], axis=0)
        rows = jnp.dot(press[...], pick, preferred_element_type=jnp.float32)
        sampled = jnp.sum(jnp.where(hit_row == cell_row, rows, 0.0), axis=0, keepdims=True)
        traction = sampled * geom_ref[0, span_pos, 0, :, where]
        strip = strips_ref[0, span_pos, :, where]
        return tuple(
            total + jnp.where(strip == base + j, traction, 0.0) for j, total in enumerate(totals)
        )

    totals = lax.fori_loop(
        0,
        deck // width,
        deck_step,
        tuple(jnp.zeros((3, width), jnp.float32) for _ in range(strip_share)),
    )
    part_force = jnp.zeros((1, n_modes), jnp.float32)
    for j in range(strip_share):
        force = jnp.sum(totals[j], axis=1, keepdims=True)
        for c in range(3):
            part_force = part_force + force[c : c + 1, :] * modes_ref[c, pl.ds(base + j, 1), :]
    md_send[...] = jnp.zeros_like(md_send)
    md_send[0:1, 0:n_modes] = part_force
    md_copies = spread(tile_peer, tiles, lambda peer: md_send, md_recv, my_tile, md_s, md_r)
    md_recv[my_tile] = md_send[...]
    for _, arrival in md_copies:
        arrival.wait_recv()
    group_force = md_recv[0]
    for t in range(1, tiles):
        group_force = group_force + md_recv[t]
    sd_send[...] = group_force
    sd_copies = spread(
        stream_peer, n_stream, lambda peer: sd_send, sd_recv, stream_pos, sd_s, sd_r
    )
    sd_recv[stream_pos] = group_force
    for copy, _ in pan_copies + co_copies + md_copies:
        copy.wait_send()
    for _, _, leave, _ in every_halo:
        leave()
    for part in range(PARTS):
        store(part).wait()
    for _, arrival in sd_copies:
        arrival.wait_recv()
    force_all = sd_recv[0]
    for t in range(1, n_stream):
        force_all = force_all + sd_recv[t]
    modal_ref[...] = force_all[0:1, 0:n_modes]
    for copy, _ in sd_copies:
        copy.wait_send()


def on_device(sizes, fields, solid, panels, owner, cells, geom, strips, modes):
    n_stream, n_span, n_vert = sizes
    tiles = n_span * n_vert
    depth, span_cells, wind = fields.shape[1:]
    half = depth // PARTS
    per_group = min(FIELDS, (wind // 2) // half)
    groups = -(-FIELDS // per_group)
    spec_cols = panels.shape[2]
    n_modes = modes.shape[2]
    plane = depth * span_cells
    f32 = jnp.float32
    dma = pltpu.SemaphoreType.DMA
    vmem = pl.BlockSpec(memory_space=pltpu.VMEM)
    anywhere = pl.BlockSpec(memory_space=pl.ANY)
    new_fields, modal = pl.pallas_call(
        functools.partial(kernel, sizes),
        out_shape=(
            jax.ShapeDtypeStruct(fields.shape, f32),
            jax.ShapeDtypeStruct((1, n_modes), f32),
        ),
        in_specs=[anywhere] + [vmem] * 7,
        out_specs=(anywhere, vmem),
        scratch_shapes=[
            pltpu.VMEM((FIELDS, depth + 2, span_cells, wind), f32),
            pltpu.VMEM((FIELDS, depth + 2, span_cells, wind), f32),
            pltpu.VMEM((FIELDS, depth, span_cells, wind), f32),
            pltpu.VMEM((2, PARTS, groups, span_cells, wind), f32),
            pltpu.VMEM((2, 2, PARTS, groups, span_cells, wind), f32),
            pltpu.VMEM((2, PARTS, groups, span_cells, wind), f32),
            pltpu.VMEM((2, 2, PARTS, FIELDS, half, wind), f32),
            pltpu.VMEM((2, 2, PARTS, FIELDS, half, wind), f32),
            pltpu.VMEM((panels.shape[0], ROWS, spec_cols), f32),
            pltpu.VMEM((tiles, ROWS, spec_cols), f32),
            pltpu.VMEM((tiles, ROWS, spec_cols), f32),
            pltpu.VMEM((ROWS, spec_cols), f32),
            pltpu.VMEM((n_stream, ROWS, spec_cols), f32),
            pltpu.VMEM((plane, spec_cols), f32),
            pltpu.VMEM((plane, ROWS), f32),
            pltpu.VMEM((plane, 2 * wind), jnp.bfloat16),
            pltpu.VMEM((ROWS, 128), f32),
            pltpu.VMEM((tiles, ROWS, 128), f32),
            pltpu.VMEM((ROWS, 128), f32),
            pltpu.VMEM((n_stream, ROWS, 128), f32),
            dma((1 + PARTS,)),
            dma((8 + 4 * PARTS,)),
            dma((8 + 4 * PARTS,)),
            dma((tiles,)),
            dma((tiles,)),
            dma((n_stream,)),
            dma((n_stream,)),
            dma((tiles,)),
            dma((tiles,)),
            dma((n_stream,)),
            dma((n_stream,)),
        ],
        compiler_params=pltpu.CompilerParams(
            collective_id=0, has_side_effects=True, vmem_limit_bytes=48 * 1024 * 1024
        ),
        name="wind_steps",
    )(fields, solid, panels, owner, cells, geom, strips, modes)
    return new_fields, modal[0]


def solution(mesh):
    sizes = tuple(mesh.shape[axis] for axis in ("stream", "span", "vert"))
    return jax.shard_map(
        functools.partial(on_device, sizes),
        mesh=mesh,
        in_specs=(
            P(None, "vert", "span", "stream"),
            P("vert", "span", "stream"),
            P(("stream", "span", "vert"), None, None),
            P(("stream", "span", "vert"), None),
            P("vert", "span", "stream", None),
            P("vert", None, "stream", None, None),
            P("vert", None, "stream", None),
            P(),
        ),
        out_specs=(P(None, "vert", "span", "stream"), P()),
        check_vma=False,
    )
```

```python
import functools
import math

import jax
import jax.numpy as jnp
from jax import lax
from jax.experimental import pallas as pl
from jax.experimental.pallas import tpu as pltpu
from jax.sharding import PartitionSpec as P

MESH = pl.DeviceIdType.MESH
HIGHEST = lax.Precision.HIGHEST

time_step = 0.15
viscous = 0.05
heat_diff = 0.03
sound_sq = 1.0
buoyant = 0.5
penalty = 0.5
relax_time = 0.5
relax_depth = 8.0
wave_cols = 16
FIELDS = 5
PARTS = 2
ONE_HOP = 64


def split_index(values, size):
    if size & (size - 1) == 0:
        return values >> (size.bit_length() - 1), values & (size - 1)
    whole = lax.div(values, jnp.int32(size))
    return whole, values - whole * size


def circle(turns):
    quarter = jnp.floor(4.0 * turns + 0.5)
    angle = (turns - 0.25 * quarter) * (2.0 * math.pi)
    sq = angle * angle
    sine = angle * (
        1.0 + sq * (-1.0 / 6 + sq * (1.0 / 120 + sq * (-1.0 / 5040 + sq * (1.0 / 362880))))
    )
    cosine = 1.0 + sq * (
        -0.5 + sq * (1.0 / 24 + sq * (-1.0 / 720 + sq * (1.0 / 40320 + sq * (-1.0 / 3628800))))
    )
    odd = (quarter == 1.0) | (quarter == 3.0)
    cos_flip = jnp.where((quarter == 1.0) | (quarter == 2.0), -1.0, 1.0)
    sin_flip = jnp.where((quarter == 2.0) | (quarter == 3.0), -1.0, 1.0)
    return cos_flip * jnp.where(odd, sine, cosine), sin_flip * jnp.where(odd, cosine, sine)


def kernel(
    sizes,
    fields_ref,
    solid_ref,
    panels_ref,
    owner_ref,
    cells_ref,
    geom_ref,
    strips_ref,
    modes_ref,
    out_ref,
    modal_ref,
    state,
    update,
    result,
    solid_in,
    owner_in,
    cells_in,
    geom_in,
    strips_in,
    modes_in,
    x_send,
    x_recv,
    x_both,
    y_send,
    y_recv,
    pan_in,
    pan_send,
    pan_recv,
    co_send,
    co_recv,
    co_rows,
    wave,
    target,
    press,
    md_send,
    md_recv,
    sd_recv,
    local_sem,
    halo_s,
    halo_r,
    pan_s,
    pan_r,
    co_s,
    co_r,
    md_s,
    md_r,
    sd_s,
    sd_r,
):
    n_stream, n_span, n_vert = sizes
    tiles = n_span * n_vert
    depth, span_cells, wind = fields_ref.shape[1:]
    half = depth // PARTS
    per_group = min(FIELDS, (wind // 2) // half)
    groups = -(-FIELDS // per_group)
    held = panels_ref.shape[1]
    spec_cols = panels_ref.shape[2]
    spec = spec_cols // 2
    strip_share = modes_ref.shape[1] // n_span
    n_modes = modes_ref.shape[2]
    deck = cells_ref.shape[3]
    me = (lax.axis_index("stream"), lax.axis_index("span"), lax.axis_index("vert"))
    stream_pos, span_pos, vert_pos = me
    my_tile = span_pos * n_vert + vert_pos

    def tile_peer(step):
        peer = lax.rem(my_tile + step, tiles)
        whole = lax.div(peer, jnp.int32(n_vert))
        return peer, (stream_pos, whole, peer - whole * n_vert)

    def stream_peer(step):
        peer = lax.rem(stream_pos + step, n_stream)
        return peer, (peer, span_pos, vert_pos)

    def any_peer(step):
        peer = lax.rem(stream_pos * tiles + my_tile + step, n_stream * tiles)
        stream = lax.div(peer, jnp.int32(tiles))
        rest = peer - stream * tiles
        whole = lax.div(rest, jnp.int32(n_vert))
        return peer, (stream, whole, rest - whole * n_vert)

    one_hop = n_stream * tiles <= ONE_HOP
    if one_hop:
        meets = [(any_peer, n_stream * tiles)]
        hops = [(any_peer, n_stream * tiles, stream_pos * tiles + my_tile)]
    else:
        meets = [(tile_peer, tiles), (stream_peer, n_stream)]
        hops = [(tile_peer, tiles, my_tile), (stream_peer, n_stream, stream_pos)]
    barrier = pltpu.get_barrier_semaphore()
    for peers, count in meets:
        for step in range(1, count):
            pl.semaphore_signal(barrier, inc=1, device_id=peers(step)[1], device_id_type=MESH)

    loads = [
        pltpu.make_async_copy(src, dst, local_sem.at[i])
        for i, (src, dst) in enumerate(
            [
                (panels_ref, pan_in),
                (owner_ref, owner_in),
                (fields_ref, state.at[:, pl.ds(1, depth)]),
                (solid_ref, solid_in),
                (cells_ref, cells_in),
                (geom_ref.at[0, span_pos], geom_in),
                (strips_ref.at[0, span_pos], strips_in),
                (modes_ref, modes_in),
            ]
        )
    ]
    for load in loads:
        load.start()

    loads[0].wait()
    loads[1].wait()
    owner = jnp.broadcast_to(owner_in[...], (tiles, held))
    wanted_by = lax.broadcasted_iota(jnp.int32, (tiles, held), 0)
    route = jnp.where(owner == wanted_by, 1.0, 0.0)
    for f in range(FIELDS):
        sums = jnp.dot(
            route, pan_in[f], precision=HIGHEST, preferred_element_type=jnp.float32
        )
        for t in range(tiles):
            pan_send[t, :, f * spec_cols : (f + 1) * spec_cols] = sums[t : t + 1, :]

    def halo(axis, way, src, dst, sem):
        count, place = sizes[axis], me[axis]
        up = way == 0
        to = lax.rem(place + (1 if up else count - 1), count)
        device = tuple(to if a == axis else me[a] for a in range(3))
        sends = place < count - 1 if up else place > 0
        gets = place > 0 if up else place < count - 1

        def copy():
            return pltpu.make_async_remote_copy(
                src_ref=src,
                dst_ref=dst,
                send_sem=halo_s.at[sem],
                recv_sem=halo_r.at[sem],
                device_id=device,
                device_id_type=MESH,
            )

        def start():
            pl.when(sends)(lambda: copy().start())

        def arrive():
            pl.when(gets)(lambda: copy().wait_recv())

        def leave():
            pl.when(sends)(lambda: copy().wait_send())

        def clear():
            @pl.when(jnp.logical_not(gets))
            def _():
                dst[...] = jnp.zeros(dst.shape, jnp.float32)

        return start, arrive, leave, clear

    z_first = [
        halo(2, 0, fields_ref.at[:, depth - 1], state.at[:, 0], 0),
        halo(2, 1, fields_ref.at[:, 0], state.at[:, depth + 1], 1),
    ]
    z_second = [
        halo(2, 0, update.at[:, depth], update.at[:, 0], 2),
        halo(2, 1, update.at[:, 1], update.at[:, depth + 1], 3),
    ]
    xy_first = [
        halo(1, way, y_send.at[0, way], y_recv.at[0, way], 4 + way) for way in range(2)
    ] + [halo(0, way, x_send.at[0], x_recv.at[0, way], 6 + way) for way in range(2)]
    xy_second = [
        [
            halo(1, way, y_send.at[1, way, part], y_recv.at[1, way, part], 8 + 4 * part + way)
            for way in range(2)
        ]
        + [
            halo(0, way, x_send.at[1, part], x_recv.at[1, way, part], 10 + 4 * part + way)
            for way in range(2)
        ]
        for part in range(PARTS)
    ]
    every_halo = z_first + z_second + xy_first + xy_second[0] + xy_second[1]

    lane = lax.broadcasted_iota(jnp.int32, (span_cells, wind), 1)
    row = lax.broadcasted_iota(jnp.int32, (span_cells, wind), 0)
    lane_pair = lane >> 1

    def pack(stage, part, z, values, held_x):
        packed = list(held_x)
        for f in range(FIELDS):
            y_send[stage, 0, part, f, pl.ds(z, 1), :] = values[f][span_cells - 1 : span_cells, :]
            y_send[stage, 1, part, f, pl.ds(z, 1), :] = values[f][0:1, :]
            pair = (f % per_group) * half + z
            turned = pltpu.roll(values[f], 2 * pair + 1, 1)
            g = f // per_group
            packed[g] = jnp.where(lane_pair == pair, turned, packed[g])
        return tuple(packed)

    no_columns = tuple(jnp.zeros((span_cells, wind), jnp.float32) for _ in range(groups))

    pl.semaphore_wait(barrier, sum(count - 1 for _, count in meets))

    def spread(peers, count, src, dst, mine, send_sem, recv_sem):
        copies = []
        for step in range(1, count):
            peer, device = peers(step)
            copy = pltpu.make_async_remote_copy(
                src_ref=src(peer),
                dst_ref=dst.at[mine],
                send_sem=send_sem.at[peer],
                recv_sem=recv_sem.at[mine],
                device_id=device,
                device_id_type=MESH,
            )
            copy.start()
            arrival = pltpu.make_async_remote_copy(
                src_ref=src(peer),
                dst_ref=dst.at[peer],
                send_sem=send_sem.at[peer],
                recv_sem=recv_sem.at[peer],
                device_id=device,
                device_id_type=MESH,
            )
            copies.append((copy, arrival))
        return copies

    pan_copies = spread(
        tile_peer, tiles, lambda peer: pan_send.at[peer], pan_recv, my_tile, pan_s, pan_r
    )
    for start, _, _, _ in z_first:
        start()
    pan_recv[my_tile] = pan_send[my_tile]
    for _, _, _, clear in every_halo:
        clear()

    loads[2].wait()
    for part in range(PARTS):

        def pack_plane(z, held_x, part=part):
            values = [state[f, 1 + part * half + z] for f in range(FIELDS)]
            return pack(0, part, z, values, held_x)

        packed = lax.fori_loop(0, half, pack_plane, no_columns, unroll=4)
        for g in range(groups):
            x_send[0, part, g] = packed[g]
    for start, _, _, _ in xy_first:
        start()

    total_z, total_y = depth * n_vert, span_cells * n_span
    period = total_y * total_z
    plane = depth * span_cells
    cell_z, cell_y = split_index(lax.broadcasted_iota(jnp.int32, (plane, spec), 0), span_cells)
    upward, across = split_index(lax.broadcasted_iota(jnp.int32, (plane, spec), 1), wave_cols)
    phase = across * (span_pos * span_cells + cell_y) * total_z
    phase = phase + upward * (vert_pos * depth + cell_z) * total_y
    phase = split_index(phase, period)[1]
    cosine, sine = circle(phase.astype(jnp.float32) * (1.0 / period))
    for i, values in enumerate((cosine, sine)):
        top = values.astype(jnp.bfloat16)
        rest = (values - top.astype(jnp.float32)).astype(jnp.bfloat16)
        wave[:, i * spec : (i + 1) * spec] = top
        wave[:, spec_cols + i * spec : spec_cols + (i + 1) * spec] = top
        wave[:, 2 * spec_cols + i * spec : 2 * spec_cols + (i + 1) * spec] = rest

    for _, arrive, _, _ in z_first + xy_first:
        arrive()
    even = (lane & 1) == 0

    def columns(stage, part):
        for g in range(groups):
            from_low = pltpu.roll(x_recv[stage, 0, part, g], 1, 1)
            from_high = pltpu.roll(x_recv[stage, 1, part, g], wind - 1, 1)
            x_both[stage, part, g] = jnp.where(even, from_high, from_low)

    for part in range(PARTS):
        columns(0, part)

    spots = stream_pos * wind + lane
    relax = jnp.where(
        spots < wind // 2, jnp.exp(spots.astype(jnp.float32) * (-1.0 / relax_depth)) / relax_time, 0.0
    )
    relax_dt = time_step * relax
    diffusion = [viscous] * 4 + [heat_diff]
    keep = {nu: 1.0 - time_step * (6.0 * nu) - relax_dt for nu in set(diffusion)}
    half_dt = 0.5 * time_step

    def inflow_term(at):
        wanted = target[pl.ds(pl.multiple_of(at * span_cells, span_cells), span_cells), :]
        return [
            relax_dt * jnp.broadcast_to(wanted[:, f : f + 1], (span_cells, wind))
            for f in range(FIELDS)
        ]

    def advance(source, stage, part, z, inflow=True):
        at = part * half + z
        terms = inflow_term(at) if inflow else None
        centre = [source[f, 1 + at] for f in range(FIELDS)]
        u, v, w = (half_dt * centre[f] for f in range(3))
        diff_x, diff_y, diff_z, new = [], [], [], []
        for f in range(FIELDS):
            c = centre[f]
            pair = (f % per_group) * half + z
            side = pltpu.roll(x_both[stage, part, f // per_group], wind - 1 - 2 * pair, 1)
            west = jnp.where(lane == 0, side, pltpu.roll(c, 1, 1))
            east = jnp.where(lane == wind - 1, side, pltpu.roll(c, wind - 1, 1))
            low = jnp.broadcast_to(y_recv[stage, 0, part, f, pl.ds(z, 1), :], c.shape)
            high = jnp.broadcast_to(y_recv[stage, 1, part, f, pl.ds(z, 1), :], c.shape)
            south = jnp.where(row == 0, low, pltpu.roll(c, 1, 0))
            north = jnp.where(row == span_cells - 1, high, pltpu.roll(c, span_cells - 1, 0))
            lower = source[f, at]
            upper = source[f, at + 2]
            dx, dy, dz = east - west, north - south, upper - lower
            around = (east + west) + (north + south) + (upper + lower)
            nu = diffusion[f]
            value = keep[nu] * c + (time_step * nu) * around
            if inflow:
                value = value + terms[f]
            value = value - (u * dx + v * dy + w * dz)
            diff_x.append(dx)
            diff_y.append(dy)
            diff_z.append(dz)
            new.append(value)
        damping = (2.0 / penalty) * solid_in[at]
        new[0] = new[0] - half_dt * diff_x[3] - damping * u
        new[1] = new[1] - half_dt * diff_y[3] - damping * v
        new[2] = new[2] - half_dt * diff_z[3] - damping * w + (time_step * buoyant) * centre[4]
        new[3] = new[3] - (half_dt * sound_sq) * (diff_x[0] + diff_y[1] + diff_z[2])
        return new

    loads[3].wait()

    def plain_plane(z, carry):
        new = advance(state, 0, 0, z, inflow=False)
        for f in range(FIELDS):
            update[f, 1 + z] = new[f]
        return carry

    lax.fori_loop(0, half // 2, plain_plane, 0, unroll=2)

    for _, arrival in pan_copies:
        arrival.wait_recv()
    mine = pan_recv[0]
    for t in range(1, tiles):
        mine = mine + pan_recv[t]
    co_send[...] = mine
    co_copies = spread(
        stream_peer, n_stream, lambda peer: co_send, co_recv, stream_pos, co_s, co_r
    )
    co_recv[stream_pos] = mine

    lax.fori_loop(half // 2, half, plain_plane, 0, unroll=2)

    for _, arrival in co_copies:
        arrival.wait_recv()
    coeffs = co_recv[0]
    for t in range(1, n_stream):
        coeffs = coeffs + co_recv[t]
    co_rows[...] = jnp.zeros_like(co_rows)
    for f in range(FIELDS):
        co_rows[f : f + 1, :] = coeffs[:, f * spec_cols : (f + 1) * spec_cols]
    top = co_rows[...].astype(jnp.bfloat16)
    rest = (co_rows[...] - top.astype(jnp.float32)).astype(jnp.bfloat16)
    inflow = lax.dot_general(
        wave[...],
        jnp.concatenate([top, rest, top], axis=1),
        (((1,), (1,)), ((), ())),
        preferred_element_type=jnp.float32,
    )
    first_field = lax.broadcasted_iota(jnp.int32, inflow.shape, 1) == 0
    target[...] = inflow + jnp.where(first_field, 1.0, 0.0)

    def finish_plane(z, held_x):
        terms = inflow_term(z)
        new = [update[f, 1 + z] + terms[f] for f in range(FIELDS)]
        for f in range(FIELDS):
            update[f, 1 + z] = new[f]
        return pack(1, 0, z, new, held_x)

    def first_plane(z, held_x):
        new = advance(state, 0, 1, z)
        for f in range(FIELDS):
            update[f, 1 + half + z] = new[f]
        return pack(1, 1, z, new, held_x)

    for part, (step_plane, turns) in enumerate(((finish_plane, 4), (first_plane, 2))):
        packed = lax.fori_loop(0, half, step_plane, no_columns, unroll=turns)
        for g in range(groups):
            x_send[1, part, g] = packed[g]
        for start, _, _, _ in xy_second[part]:
            start()
        z_second[1 - part][0]()

    def second_plane(part, z):
        new = advance(update, 1, part, z)
        at = part * half + z
        for f in range(FIELDS):
            value = 0.5 * (state[f, 1 + at] + new[f])
            result[f, at] = value
            if f == 3:
                top = value.astype(jnp.bfloat16)
                rest = (value - top.astype(jnp.float32)).astype(jnp.bfloat16)
                where = pl.ds(pl.multiple_of(at * span_cells, span_cells), span_cells)
                press[where, 0:wind] = top
                press[where, wind:] = rest

    def store(part):
        where = pl.ds(part * half, half)
        return pltpu.make_async_copy(
            result.at[:, where], out_ref.at[:, where], local_sem.at[8 + part]
        )

    for part in range(PARTS):
        for _, arrive, _, _ in xy_second[part]:
            arrive()
        columns(1, part)
        if part == PARTS - 1:
            z_second[1][1]()

        def plane_step(z, carry, part=part):
            second_plane(part, z)
            return carry

        if part == 0:
            lax.fori_loop(2, half, plane_step, 0, unroll=2)
            z_second[0][1]()
            second_plane(0, 0)
            second_plane(0, 1)
        else:
            lax.fori_loop(0, half, plane_step, 0, unroll=2)
        store(part).start()

    for load in loads[4:]:
        load.wait()
    width = min(deck, 256)
    base = span_pos * strip_share
    hit_row = lax.broadcasted_iota(jnp.int32, (plane, width), 0)
    hit_col = lax.broadcasted_iota(jnp.int32, (wind, width), 0)

    def deck_step(i, totals):
        where = pl.ds(pl.multiple_of(i * width, width), width)
        cell_row, cell_col = split_index(cells_in[0, 0, :, where], wind)
        pick = jnp.where(hit_col == cell_col, 1.0, 0.0).astype(jnp.bfloat16)
        pick = jnp.concatenate([pick, pick], axis=0)
        rows = jnp.dot(press[...], pick, preferred_element_type=jnp.float32)
        sampled = jnp.sum(jnp.where(hit_row == cell_row, rows, 0.0), axis=0, keepdims=True)
        traction = [sampled * geom_in[c, :, where] for c in range(3)]
        strip = strips_in[:, where]
        return tuple(
            total + jnp.where(strip == base + n // 3, traction[n % 3], 0.0)
            for n, total in enumerate(totals)
        )

    totals = lax.fori_loop(
        0,
        deck // width,
        deck_step,
        tuple(jnp.zeros((1, width), jnp.float32) for _ in range(3 * strip_share)),
        unroll=2,
    )
    force = jnp.sum(jnp.concatenate(totals, axis=0), axis=1, keepdims=True)
    shapes = jnp.concatenate(
        [modes_in[n % 3, pl.ds(base + n // 3, 1), :] for n in range(3 * strip_share)], axis=0
    )
    part_force = jnp.sum(force * shapes, axis=0, keepdims=True)
    md_copies = []
    slots = ((md_recv, md_s, md_r), (sd_recv, sd_s, sd_r))
    for hop, (peers, count, mine) in enumerate(hops):
        recv, send_sem, recv_sem = slots[hop]
        md_send[hop] = jnp.zeros(md_send.shape[1:], jnp.float32)
        md_send[hop, :, 0:n_modes] = part_force
        copies = spread(
            peers, count, lambda peer, hop=hop: md_send.at[hop], recv, mine, send_sem, recv_sem
        )
        recv[mine] = md_send[hop]
        if hop == 0:
            for copy, _ in pan_copies + co_copies:
                copy.wait_send()
            for _, _, leave, _ in every_halo:
                leave()
            for part in range(PARTS):
                store(part).wait()
        for _, arrival in copies:
            arrival.wait_recv()
        total = recv[0]
        for t in range(1, count):
            total = total + recv[t]
        part_force = total[:, 0:n_modes]
        md_copies = md_copies + copies
    modal_ref[...] = part_force
    for copy, _ in md_copies:
        copy.wait_send()


def on_device(sizes, fields, solid, panels, owner, cells, geom, strips, modes):
    n_stream, n_span, n_vert = sizes
    tiles = n_span * n_vert
    depth, span_cells, wind = fields.shape[1:]
    half = depth // PARTS
    per_group = min(FIELDS, (wind // 2) // half)
    groups = -(-FIELDS // per_group)
    spec_cols = panels.shape[2]
    n_modes = modes.shape[2]
    plane = depth * span_cells
    f32 = jnp.float32
    dma = pltpu.SemaphoreType.DMA
    vmem = pl.BlockSpec(memory_space=pltpu.VMEM)
    hbm = pl.BlockSpec(memory_space=pltpu.HBM)
    held = panels.shape[0]
    if n_stream * tiles <= ONE_HOP:
        first_hop, second_hop = n_stream * tiles, 1
    else:
        first_hop, second_hop = tiles, n_stream
    panels = panels.transpose(1, 0, 2)
    owner = owner.reshape(1, held)
    geom = geom.transpose(0, 1, 3, 2, 4)
    new_fields, modal = pl.pallas_call(
        functools.partial(kernel, sizes),
        out_shape=(
            jax.ShapeDtypeStruct(fields.shape, f32),
            jax.ShapeDtypeStruct((1, n_modes), f32),
        ),
        in_specs=[hbm] * 8,
        out_specs=(hbm, vmem),
        scratch_shapes=[
            pltpu.VMEM((FIELDS, depth + 2, span_cells, wind), f32),
            pltpu.VMEM((FIELDS, depth + 2, span_cells, wind), f32),
            pltpu.VMEM((FIELDS, depth, span_cells, wind), f32),
            pltpu.VMEM(solid.shape, f32),
            pltpu.VMEM(owner.shape, jnp.int32),
            pltpu.VMEM(cells.shape, jnp.int32),
            pltpu.VMEM(geom.shape[2:], f32),
            pltpu.VMEM(strips.shape[2:], jnp.int32),
            pltpu.VMEM(modes.shape, f32),
            pltpu.VMEM((2, PARTS, groups, span_cells, wind), f32),
            pltpu.VMEM((2, 2, PARTS, groups, span_cells, wind), f32),
            pltpu.VMEM((2, PARTS, groups, span_cells, wind), f32),
            pltpu.VMEM((2, 2, PARTS, FIELDS, half, wind), f32),
            pltpu.VMEM((2, 2, PARTS, FIELDS, half, wind), f32),
            pltpu.VMEM(panels.shape, f32),
            pltpu.VMEM((tiles, 1, FIELDS * spec_cols), f32),
            pltpu.VMEM((tiles, 1, FIELDS * spec_cols), f32),
            pltpu.VMEM((1, FIELDS * spec_cols), f32),
            pltpu.VMEM((n_stream, 1, FIELDS * spec_cols), f32),
            pltpu.VMEM((16, spec_cols), f32),
            pltpu.VMEM((plane, 3 * spec_cols), jnp.bfloat16),
            pltpu.VMEM((plane, 16), f32),
            pltpu.VMEM((plane, 2 * wind), jnp.bfloat16),
            pltpu.VMEM((2, 1, 128), f32),
            pltpu.VMEM((first_hop, 1, 128), f32),
            pltpu.VMEM((second_hop, 1, 128), f32),
            dma((8 + PARTS,)),
            dma((8 + 4 * PARTS,)),
            dma((8 + 4 * PARTS,)),
            dma((tiles,)),
            dma((tiles,)),
            dma((n_stream,)),
            dma((n_stream,)),
            dma((first_hop,)),
            dma((first_hop,)),
            dma((second_hop,)),
            dma((second_hop,)),
        ],
        compiler_params=pltpu.CompilerParams(
            collective_id=0, has_side_effects=True, vmem_limit_bytes=63 * 1024 * 1024
        ),
        name="wind_steps",
    )(fields, solid, panels, owner, cells, geom, strips, modes)
    return new_fields, modal[0]


def solution(mesh):
    sizes = tuple(mesh.shape[axis] for axis in ("stream", "span", "vert"))
    return jax.shard_map(
        functools.partial(on_device, sizes),
        mesh=mesh,
        in_specs=(
            P(None, "vert", "span", "stream"),
            P("vert", "span", "stream"),
            P(("stream", "span", "vert"), None, None),
            P(("stream", "span", "vert"), None),
            P("vert", "span", "stream", None),
            P("vert", None, "stream", None, None),
            P("vert", None, "stream", None),
            P(),
        ),
        out_specs=(P(None, "vert", "span", "stream"), P()),
        check_vma=False,
    )
```

```python
import functools
import math

import jax
import jax.numpy as jnp
from jax import lax
from jax.experimental import pallas as pl
from jax.experimental.pallas import tpu as pltpu
from jax.sharding import PartitionSpec as P

MESH = pl.DeviceIdType.MESH
HIGHEST = lax.Precision.HIGHEST

time_step = 0.15
viscous = 0.05
heat_diff = 0.03
sound_sq = 1.0
buoyant = 0.5
penalty = 0.5
relax_time = 0.5
relax_depth = 8.0
wave_cols = 16
FIELDS = 5
PARTS = 2
ONE_HOP = 64


def split_index(values, size):
    if size & (size - 1) == 0:
        return values >> (size.bit_length() - 1), values & (size - 1)
    whole = lax.div(values, jnp.int32(size))
    return whole, values - whole * size


def circle(turns):
    quarter = jnp.floor(4.0 * turns + 0.5)
    angle = (turns - 0.25 * quarter) * (2.0 * math.pi)
    sq = angle * angle
    sine = angle * (
        1.0 + sq * (-1.0 / 6 + sq * (1.0 / 120 + sq * (-1.0 / 5040 + sq * (1.0 / 362880))))
    )
    cosine = 1.0 + sq * (
        -0.5 + sq * (1.0 / 24 + sq * (-1.0 / 720 + sq * (1.0 / 40320 + sq * (-1.0 / 3628800))))
    )
    odd = (quarter == 1.0) | (quarter == 3.0)
    cos_flip = jnp.where((quarter == 1.0) | (quarter == 2.0), -1.0, 1.0)
    sin_flip = jnp.where((quarter == 2.0) | (quarter == 3.0), -1.0, 1.0)
    return cos_flip * jnp.where(odd, sine, cosine), sin_flip * jnp.where(odd, cosine, sine)


def kernel(
    sizes,
    fields_ref,
    solid_ref,
    panels_ref,
    owner_ref,
    cells_ref,
    geom_ref,
    strips_ref,
    modes_ref,
    out_ref,
    modal_ref,
    state,
    update,
    result,
    solid_in,
    owner_in,
    cells_in,
    geom_in,
    strips_in,
    modes_in,
    x_send,
    x_recv,
    x_both,
    y_send,
    y_recv,
    pan_in,
    pan_send,
    pan_recv,
    co_send,
    co_recv,
    co_rows,
    wave,
    target,
    press,
    md_send,
    md_recv,
    sd_recv,
    local_sem,
    halo_s,
    halo_r,
    pan_s,
    pan_r,
    co_s,
    co_r,
    md_s,
    md_r,
    sd_s,
    sd_r,
):
    n_stream, n_span, n_vert = sizes
    tiles = n_span * n_vert
    depth, span_cells, wind = fields_ref.shape[1:]
    half = depth // PARTS
    per_group = min(FIELDS, (wind // 2) // half)
    groups = -(-FIELDS // per_group)
    held = panels_ref.shape[1]
    spec_cols = panels_ref.shape[2]
    spec = spec_cols // 2
    strip_share = modes_ref.shape[1] // n_span
    n_modes = modes_ref.shape[2]
    deck = cells_ref.shape[3]
    me = (lax.axis_index("stream"), lax.axis_index("span"), lax.axis_index("vert"))
    stream_pos, span_pos, vert_pos = me
    my_tile = span_pos * n_vert + vert_pos

    def tile_peer(step):
        peer = lax.rem(my_tile + step, tiles)
        whole = lax.div(peer, jnp.int32(n_vert))
        return peer, (stream_pos, whole, peer - whole * n_vert)

    def stream_peer(step):
        peer = lax.rem(stream_pos + step, n_stream)
        return peer, (peer, span_pos, vert_pos)

    def any_peer(step):
        peer = lax.rem(stream_pos * tiles + my_tile + step, n_stream * tiles)
        stream = lax.div(peer, jnp.int32(tiles))
        rest = peer - stream * tiles
        whole = lax.div(rest, jnp.int32(n_vert))
        return peer, (stream, whole, rest - whole * n_vert)

    one_hop = n_stream * tiles <= ONE_HOP
    if one_hop:
        meets = [(any_peer, n_stream * tiles)]
        hops = [(any_peer, n_stream * tiles, stream_pos * tiles + my_tile)]
    else:
        meets = [(tile_peer, tiles), (stream_peer, n_stream)]
        hops = [(tile_peer, tiles, my_tile), (stream_peer, n_stream, stream_pos)]
    barrier = pltpu.get_barrier_semaphore()
    for peers, count in meets:
        for step in range(1, count):
            pl.semaphore_signal(barrier, inc=1, device_id=peers(step)[1], device_id_type=MESH)

    loads = [
        pltpu.make_async_copy(src, dst, local_sem.at[i])
        for i, (src, dst) in enumerate(
            [
                (fields_ref, state.at[:, pl.ds(1, depth)]),
                (panels_ref, pan_in),
                (owner_ref, owner_in),
                (solid_ref, solid_in),
                (cells_ref, cells_in),
                (geom_ref.at[0, span_pos], geom_in),
                (strips_ref.at[0, span_pos], strips_in),
                (modes_ref, modes_in),
            ]
        )
    ]
    for load in loads:
        load.start()

    def halo(axis, way, src, dst, sem):
        count, place = sizes[axis], me[axis]
        up = way == 0
        to = lax.rem(place + (1 if up else count - 1), count)
        device = tuple(to if a == axis else me[a] for a in range(3))
        sends = place < count - 1 if up else place > 0
        gets = place > 0 if up else place < count - 1

        def copy():
            return pltpu.make_async_remote_copy(
                src_ref=src,
                dst_ref=dst,
                send_sem=halo_s.at[sem],
                recv_sem=halo_r.at[sem],
                device_id=device,
                device_id_type=MESH,
            )

        def start():
            pl.when(sends)(lambda: copy().start())

        def arrive():
            pl.when(gets)(lambda: copy().wait_recv())

        def leave():
            pl.when(sends)(lambda: copy().wait_send())

        def clear():
            @pl.when(jnp.logical_not(gets))
            def _():
                dst[...] = jnp.zeros(dst.shape, jnp.float32)

        return start, arrive, leave, clear

    z_first = [
        halo(2, 0, fields_ref.at[:, depth - 1], state.at[:, 0], 0),
        halo(2, 1, fields_ref.at[:, 0], state.at[:, depth + 1], 1),
    ]
    z_second = [
        halo(2, 0, update.at[:, depth], update.at[:, 0], 2),
        halo(2, 1, update.at[:, 1], update.at[:, depth + 1], 3),
    ]
    xy_first = [
        halo(1, way, y_send.at[0, way], y_recv.at[0, way], 4 + way) for way in range(2)
    ] + [halo(0, way, x_send.at[0], x_recv.at[0, way], 6 + way) for way in range(2)]
    xy_second = [
        [
            halo(1, way, y_send.at[1, way, part], y_recv.at[1, way, part], 8 + 4 * part + way)
            for way in range(2)
        ]
        + [
            halo(0, way, x_send.at[1, part], x_recv.at[1, way, part], 10 + 4 * part + way)
            for way in range(2)
        ]
        for part in range(PARTS)
    ]
    every_halo = z_first + z_second + xy_first + xy_second[0] + xy_second[1]

    lane = lax.broadcasted_iota(jnp.int32, (span_cells, wind), 1)
    row = lax.broadcasted_iota(jnp.int32, (span_cells, wind), 0)
    lane_pair = lane >> 1

    def pack(stage, part, z, values, held_x):
        packed = list(held_x)
        for f in range(FIELDS):
            y_send[stage, 0, part, f, pl.ds(z, 1), :] = values[f][span_cells - 1 : span_cells, :]
            y_send[stage, 1, part, f, pl.ds(z, 1), :] = values[f][0:1, :]
            pair = (f % per_group) * half + z
            turned = pltpu.roll(values[f], 2 * pair + 1, 1)
            g = f // per_group
            packed[g] = jnp.where(lane_pair == pair, turned, packed[g])
        return tuple(packed)

    no_columns = tuple(jnp.zeros((span_cells, wind), jnp.float32) for _ in range(groups))

    def spread(peers, count, src, dst, mine, send_sem, recv_sem):
        copies = []
        for step in range(1, count):
            peer, device = peers(step)
            copy = pltpu.make_async_remote_copy(
                src_ref=src(peer),
                dst_ref=dst.at[mine],
                send_sem=send_sem.at[peer],
                recv_sem=recv_sem.at[mine],
                device_id=device,
                device_id_type=MESH,
            )
            copy.start()
            arrival = pltpu.make_async_remote_copy(
                src_ref=src(peer),
                dst_ref=dst.at[peer],
                send_sem=send_sem.at[peer],
                recv_sem=recv_sem.at[peer],
                device_id=device,
                device_id_type=MESH,
            )
            copies.append((copy, arrival))
        return copies

    loads[0].wait()
    for part in range(PARTS):

        def pack_plane(z, held_x, part=part):
            values = [state[f, 1 + part * half + z] for f in range(FIELDS)]
            return pack(0, part, z, values, held_x)

        packed = lax.fori_loop(0, half, pack_plane, no_columns, unroll=4)
        for g in range(groups):
            x_send[0, part, g] = packed[g]
    pl.semaphore_wait(barrier, sum(count - 1 for _, count in meets))
    for start, _, _, _ in z_first + xy_first:
        start()
    for _, _, _, clear in every_halo:
        clear()

    loads[1].wait()
    loads[2].wait()
    owner = jnp.broadcast_to(owner_in[...], (tiles, held))
    wanted_by = lax.broadcasted_iota(jnp.int32, (tiles, held), 0)
    route = jnp.where(owner == wanted_by, 1.0, 0.0)
    for f in range(FIELDS):
        sums = jnp.dot(
            route, pan_in[f], precision=HIGHEST, preferred_element_type=jnp.float32
        )
        for t in range(tiles):
            pan_send[t, :, f * spec_cols : (f + 1) * spec_cols] = sums[t : t + 1, :]

    pan_copies = spread(
        tile_peer, tiles, lambda peer: pan_send.at[peer], pan_recv, my_tile, pan_s, pan_r
    )
    pan_recv[my_tile] = pan_send[my_tile]

    total_z, total_y = depth * n_vert, span_cells * n_span
    period = total_y * total_z
    plane = depth * span_cells
    cell_z, cell_y = split_index(lax.broadcasted_iota(jnp.int32, (plane, spec), 0), span_cells)
    upward, across = split_index(lax.broadcasted_iota(jnp.int32, (plane, spec), 1), wave_cols)
    phase = across * (span_pos * span_cells + cell_y) * total_z
    phase = phase + upward * (vert_pos * depth + cell_z) * total_y
    phase = split_index(phase, period)[1]
    cosine, sine = circle(phase.astype(jnp.float32) * (1.0 / period))
    for i, values in enumerate((cosine, sine)):
        top = values.astype(jnp.bfloat16)
        rest = (values - top.astype(jnp.float32)).astype(jnp.bfloat16)
        wave[:, i * spec : (i + 1) * spec] = top
        wave[:, spec_cols + i * spec : spec_cols + (i + 1) * spec] = top
        wave[:, 2 * spec_cols + i * spec : 2 * spec_cols + (i + 1) * spec] = rest

    for _, arrive, _, _ in z_first + xy_first:
        arrive()
    even = (lane & 1) == 0

    def columns(stage, part):
        for g in range(groups):
            from_low = pltpu.roll(x_recv[stage, 0, part, g], 1, 1)
            from_high = pltpu.roll(x_recv[stage, 1, part, g], wind - 1, 1)
            x_both[stage, part, g] = jnp.where(even, from_high, from_low)

    for part in range(PARTS):
        columns(0, part)

    spots = stream_pos * wind + lane
    relax = jnp.where(
        spots < wind // 2, jnp.exp(spots.astype(jnp.float32) * (-1.0 / relax_depth)) / relax_time, 0.0
    )
    relax_dt = time_step * relax
    diffusion = [viscous] * 4 + [heat_diff]
    keep = {nu: 1.0 - time_step * (6.0 * nu) - relax_dt for nu in set(diffusion)}
    half_dt = 0.5 * time_step

    every_field = tuple(range(FIELDS))

    def inflow_term(at, only):
        wanted = target[pl.ds(pl.multiple_of(at * span_cells, span_cells), span_cells), :]
        return {
            f: relax_dt * jnp.broadcast_to(wanted[:, f : f + 1], (span_cells, wind))
            for f in only
        }

    def advance(source, stage, part, z, inflow=True, only=every_field):
        at = part * half + z
        terms = inflow_term(at, only) if inflow else None
        centre = [source[f, 1 + at] for f in range(FIELDS)]
        u, v, w = (half_dt * centre[f] for f in range(3))
        sides = {}

        def x_sides(f):
            if ("x", f) not in sides:
                c = centre[f]
                pair = (f % per_group) * half + z
                side = pltpu.roll(x_both[stage, part, f // per_group], wind - 1 - 2 * pair, 1)
                west = jnp.where(lane == 0, side, pltpu.roll(c, 1, 1))
                east = jnp.where(lane == wind - 1, side, pltpu.roll(c, wind - 1, 1))
                sides["x", f] = east - west, east + west
            return sides["x", f]

        def y_sides(f):
            if ("y", f) not in sides:
                c = centre[f]
                low = jnp.broadcast_to(y_recv[stage, 0, part, f, pl.ds(z, 1), :], c.shape)
                high = jnp.broadcast_to(y_recv[stage, 1, part, f, pl.ds(z, 1), :], c.shape)
                south = jnp.where(row == 0, low, pltpu.roll(c, 1, 0))
                north = jnp.where(row == span_cells - 1, high, pltpu.roll(c, span_cells - 1, 0))
                sides["y", f] = north - south, north + south
            return sides["y", f]

        def z_sides(f):
            if ("z", f) not in sides:
                lower, upper = source[f, at], source[f, at + 2]
                sides["z", f] = upper - lower, upper + lower
            return sides["z", f]

        damping = (2.0 / penalty) * solid_in[at] if only != (3,) else None
        new = {}
        for f in only:
            (dx, sum_x), (dy, sum_y), (dz, sum_z) = x_sides(f), y_sides(f), z_sides(f)
            nu = diffusion[f]
            value = keep[nu] * centre[f] + (time_step * nu) * (sum_x + sum_y + sum_z)
            if inflow:
                value = value + terms[f]
            new[f] = value - (u * dx + v * dy + w * dz)
        for f, sided, speed in ((0, x_sides, u), (1, y_sides, v), (2, z_sides, w)):
            if f in new:
                new[f] = new[f] - half_dt * sided(3)[0] - damping * speed
        if 2 in new:
            new[2] = new[2] + (time_step * buoyant) * centre[4]
        if 3 in new:
            spread_out = x_sides(0)[0] + y_sides(1)[0] + z_sides(2)[0]
            new[3] = new[3] - (half_dt * sound_sq) * spread_out
        return new

    loads[3].wait()

    def plain_plane(z, carry):
        new = advance(state, 0, 0, z, inflow=False)
        for f in range(FIELDS):
            update[f, 1 + z] = new[f]
        return carry

    lax.fori_loop(0, half // 2, plain_plane, 0, unroll=2)

    for _, arrival in pan_copies:
        arrival.wait_recv()
    mine = pan_recv[0]
    for t in range(1, tiles):
        mine = mine + pan_recv[t]
    co_send[...] = mine
    co_copies = spread(
        stream_peer, n_stream, lambda peer: co_send, co_recv, stream_pos, co_s, co_r
    )
    co_recv[stream_pos] = mine

    lax.fori_loop(half // 2, half, plain_plane, 0, unroll=2)

    for _, arrival in co_copies:
        arrival.wait_recv()
    coeffs = co_recv[0]
    for t in range(1, n_stream):
        coeffs = coeffs + co_recv[t]
    co_rows[...] = jnp.zeros_like(co_rows)
    for f in range(FIELDS):
        co_rows[f : f + 1, :] = coeffs[:, f * spec_cols : (f + 1) * spec_cols]
    top = co_rows[...].astype(jnp.bfloat16)
    rest = (co_rows[...] - top.astype(jnp.float32)).astype(jnp.bfloat16)
    inflow = lax.dot_general(
        wave[...],
        jnp.concatenate([top, rest, top], axis=1),
        (((1,), (1,)), ((), ())),
        preferred_element_type=jnp.float32,
    )
    first_field = lax.broadcasted_iota(jnp.int32, inflow.shape, 1) == 0
    target[...] = inflow + jnp.where(first_field, 1.0, 0.0)

    def finish_plane(z, held_x):
        terms = inflow_term(z, every_field)
        new = [update[f, 1 + z] + terms[f] for f in range(FIELDS)]
        for f in range(FIELDS):
            update[f, 1 + z] = new[f]
        return pack(1, 0, z, new, held_x)

    def first_plane(z, held_x):
        new = advance(state, 0, 1, z)
        for f in range(FIELDS):
            update[f, 1 + half + z] = new[f]
        return pack(1, 1, z, new, held_x)

    for part, (step_plane, turns) in enumerate(((finish_plane, 4), (first_plane, 2))):
        packed = lax.fori_loop(0, half, step_plane, no_columns, unroll=turns)
        for g in range(groups):
            x_send[1, part, g] = packed[g]
        for start, _, _, _ in xy_second[part]:
            start()
        z_second[1 - part][0]()

    def second_plane(part, z, only=every_field):
        new = advance(update, 1, part, z, only=only)
        at = part * half + z
        for f in only:
            value = 0.5 * (state[f, 1 + at] + new[f])
            result[f, at] = value
            if f == 3:
                top = value.astype(jnp.bfloat16)
                rest = (value - top.astype(jnp.float32)).astype(jnp.bfloat16)
                where = pl.ds(pl.multiple_of(at * span_cells, span_cells), span_cells)
                press[where, 0:wind] = top
                press[where, wind:] = rest

    def store(part):
        where = pl.ds(part * half, half)
        return pltpu.make_async_copy(
            result.at[:, where], out_ref.at[:, where], local_sem.at[8 + part]
        )

    for part in range(PARTS):
        for _, arrive, _, _ in xy_second[part]:
            arrive()
        columns(1, part)
        if part == PARTS - 1:
            z_second[1][1]()

        def plane_step(z, carry, part=part):
            second_plane(part, z, every_field if part == 0 else (3,))
            return carry

        if part == 0:
            lax.fori_loop(2, half, plane_step, 0, unroll=2)
            z_second[0][1]()
            second_plane(0, 0)
            second_plane(0, 1)
            store(0).start()
        else:
            lax.fori_loop(0, half, plane_step, 0, unroll=4)

    for load in loads[4:]:
        load.wait()
    width = min(deck, 256)
    base = span_pos * strip_share
    hit_row = lax.broadcasted_iota(jnp.int32, (plane, width), 0)
    hit_col = lax.broadcasted_iota(jnp.int32, (wind, width), 0)

    def deck_step(i, totals):
        where = pl.ds(pl.multiple_of(i * width, width), width)
        cell_row, cell_col = split_index(cells_in[0, 0, :, where], wind)
        pick = jnp.where(hit_col == cell_col, 1.0, 0.0).astype(jnp.bfloat16)
        pick = jnp.concatenate([pick, pick], axis=0)
        rows = jnp.dot(press[...], pick, preferred_element_type=jnp.float32)
        sampled = jnp.sum(jnp.where(hit_row == cell_row, rows, 0.0), axis=0, keepdims=True)
        traction = [sampled * geom_in[c, :, where] for c in range(3)]
        strip = strips_in[:, where]
        return tuple(
            total + jnp.where(strip == base + n // 3, traction[n % 3], 0.0)
            for n, total in enumerate(totals)
        )

    totals = lax.fori_loop(
        0,
        deck // width,
        deck_step,
        tuple(jnp.zeros((1, width), jnp.float32) for _ in range(3 * strip_share)),
        unroll=2,
    )
    force = jnp.sum(jnp.concatenate(totals, axis=0), axis=1, keepdims=True)
    shapes = jnp.concatenate(
        [modes_in[n % 3, pl.ds(base + n // 3, 1), :] for n in range(3 * strip_share)], axis=0
    )
    part_force = jnp.sum(force * shapes, axis=0, keepdims=True)

    def other_fields(z, carry):
        second_plane(1, z, (0, 1, 2, 4))
        return carry

    md_copies = []
    slots = ((md_recv, md_s, md_r), (sd_recv, sd_s, sd_r))
    for hop, (peers, count, mine) in enumerate(hops):
        recv, send_sem, recv_sem = slots[hop]
        md_send[hop] = jnp.zeros(md_send.shape[1:], jnp.float32)
        md_send[hop, :, 0:n_modes] = part_force
        copies = spread(
            peers, count, lambda peer, hop=hop: md_send.at[hop], recv, mine, send_sem, recv_sem
        )
        recv[mine] = md_send[hop]
        if hop == 0:
            lax.fori_loop(0, half, other_fields, 0, unroll=2)
            store(1).start()
            for copy, _ in pan_copies + co_copies:
                copy.wait_send()
            for _, _, leave, _ in every_halo:
                leave()
            for part in range(PARTS):
                store(part).wait()
        for _, arrival in copies:
            arrival.wait_recv()
        total = recv[0]
        for t in range(1, count):
            total = total + recv[t]
        part_force = total[:, 0:n_modes]
        md_copies = md_copies + copies
    modal_ref[...] = part_force
    for copy, _ in md_copies:
        copy.wait_send()


def place(fields_ref, modal_ref, out_ref, force_ref, held, force, in_sem, out_sem):
    count = fields_ref.shape[0]
    pieces = [(modal_ref, force, force_ref)]
    pieces += [(fields_ref.at[f], held.at[f], out_ref.at[f]) for f in range(count)]
    comes = [
        pltpu.make_async_copy(src, mid, in_sem.at[i]) for i, (src, mid, _) in enumerate(pieces)
    ]
    goes = [
        pltpu.make_async_copy(mid, dst, out_sem.at[i]) for i, (_, mid, dst) in enumerate(pieces)
    ]
    for come in comes:
        come.start()
    for come, go in zip(comes, goes):
        come.wait()
        go.start()
    for go in goes:
        go.wait()


def on_device(sizes, fields, solid, panels, owner, cells, geom, strips, modes):
    n_stream, n_span, n_vert = sizes
    tiles = n_span * n_vert
    depth, span_cells, wind = fields.shape[1:]
    half = depth // PARTS
    per_group = min(FIELDS, (wind // 2) // half)
    groups = -(-FIELDS // per_group)
    spec_cols = panels.shape[2]
    n_modes = modes.shape[2]
    plane = depth * span_cells
    f32 = jnp.float32
    dma = pltpu.SemaphoreType.DMA
    vmem = pl.BlockSpec(memory_space=pltpu.VMEM)
    hbm = pl.BlockSpec(memory_space=pltpu.HBM)
    held = panels.shape[0]
    if n_stream * tiles <= ONE_HOP:
        first_hop, second_hop = n_stream * tiles, 1
    else:
        first_hop, second_hop = tiles, n_stream
    panels = panels.transpose(1, 0, 2)
    owner = owner.reshape(1, held)
    geom = geom.transpose(0, 1, 3, 2, 4)
    new_fields, modal = pl.pallas_call(
        functools.partial(kernel, sizes),
        out_shape=(
            jax.ShapeDtypeStruct(fields.shape, f32),
            jax.ShapeDtypeStruct((1, n_modes), f32),
        ),
        in_specs=[hbm] * 8,
        out_specs=(hbm, vmem),
        scratch_shapes=[
            pltpu.VMEM((FIELDS, depth + 2, span_cells, wind), f32),
            pltpu.VMEM((FIELDS, depth + 2, span_cells, wind), f32),
            pltpu.VMEM((FIELDS, depth, span_cells, wind), f32),
            pltpu.VMEM(solid.shape, f32),
            pltpu.VMEM(owner.shape, jnp.int32),
            pltpu.VMEM(cells.shape, jnp.int32),
            pltpu.VMEM(geom.shape[2:], f32),
            pltpu.VMEM(strips.shape[2:], jnp.int32),
            pltpu.VMEM(modes.shape, f32),
            pltpu.VMEM((2, PARTS, groups, span_cells, wind), f32),
            pltpu.VMEM((2, 2, PARTS, groups, span_cells, wind), f32),
            pltpu.VMEM((2, PARTS, groups, span_cells, wind), f32),
            pltpu.VMEM((2, 2, PARTS, FIELDS, half, wind), f32),
            pltpu.VMEM((2, 2, PARTS, FIELDS, half, wind), f32),
            pltpu.VMEM(panels.shape, f32),
            pltpu.VMEM((tiles, 1, FIELDS * spec_cols), f32),
            pltpu.VMEM((tiles, 1, FIELDS * spec_cols), f32),
            pltpu.VMEM((1, FIELDS * spec_cols), f32),
            pltpu.VMEM((n_stream, 1, FIELDS * spec_cols), f32),
            pltpu.VMEM((16, spec_cols), f32),
            pltpu.VMEM((plane, 3 * spec_cols), jnp.bfloat16),
            pltpu.VMEM((plane, 16), f32),
            pltpu.VMEM((plane, 2 * wind), jnp.bfloat16),
            pltpu.VMEM((2, 1, 128), f32),
            pltpu.VMEM((first_hop, 1, 128), f32),
            pltpu.VMEM((second_hop, 1, 128), f32),
            dma((8 + PARTS,)),
            dma((8 + 4 * PARTS,)),
            dma((8 + 4 * PARTS,)),
            dma((tiles,)),
            dma((tiles,)),
            dma((n_stream,)),
            dma((n_stream,)),
            dma((first_hop,)),
            dma((first_hop,)),
            dma((second_hop,)),
            dma((second_hop,)),
        ],
        compiler_params=pltpu.CompilerParams(
            collective_id=0, has_side_effects=True, vmem_limit_bytes=63 * 1024 * 1024
        ),
        name="wind_steps",
    )(fields, solid, panels, owner, cells, geom, strips, modes)
    new_fields, modal = pl.pallas_call(
        place,
        out_shape=(
            jax.ShapeDtypeStruct(fields.shape, f32),
            jax.ShapeDtypeStruct((1, n_modes), f32),
        ),
        in_specs=[hbm, hbm],
        out_specs=(hbm, hbm),
        scratch_shapes=[
            pltpu.VMEM(fields.shape, f32),
            pltpu.VMEM((1, n_modes), f32),
            dma((FIELDS + 1,)),
            dma((FIELDS + 1,)),
        ],
        compiler_params=pltpu.CompilerParams(vmem_limit_bytes=63 * 1024 * 1024),
        name="place_results",
    )(new_fields, modal)
    return new_fields, modal[0]


def solution(mesh):
    sizes = tuple(mesh.shape[axis] for axis in ("stream", "span", "vert"))
    return jax.shard_map(
        functools.partial(on_device, sizes),
        mesh=mesh,
        in_specs=(
            P(None, "vert", "span", "stream"),
            P("vert", "span", "stream"),
            P(("stream", "span", "vert"), None, None),
            P(("stream", "span", "vert"), None),
            P("vert", "span", "stream", None),
            P("vert", None, "stream", None, None),
            P("vert", None, "stream", None),
            P(),
        ),
        out_specs=(P(None, "vert", "span", "stream"), P()),
        check_vma=False,
    )
```

```python
import functools
import math

import jax
import jax.numpy as jnp
from jax import lax
from jax.experimental import pallas as pl
from jax.experimental.pallas import tpu as pltpu
from jax.sharding import PartitionSpec as P

MESH = pl.DeviceIdType.MESH
HIGHEST = lax.Precision.HIGHEST

time_step = 0.15
viscous = 0.05
heat_diff = 0.03
sound_sq = 1.0
buoyant = 0.5
penalty = 0.5
relax_time = 0.5
relax_depth = 8.0
wave_cols = 16
FIELDS = 5
PARTS = 2
ONE_HOP = 64


def split_index(values, size):
    if size & (size - 1) == 0:
        return values >> (size.bit_length() - 1), values & (size - 1)
    whole = lax.div(values, jnp.int32(size))
    return whole, values - whole * size


def circle(turns):
    quarter = jnp.floor(4.0 * turns + 0.5)
    angle = (turns - 0.25 * quarter) * (2.0 * math.pi)
    sq = angle * angle
    sine = angle * (
        1.0 + sq * (-1.0 / 6 + sq * (1.0 / 120 + sq * (-1.0 / 5040 + sq * (1.0 / 362880))))
    )
    cosine = 1.0 + sq * (
        -0.5 + sq * (1.0 / 24 + sq * (-1.0 / 720 + sq * (1.0 / 40320 + sq * (-1.0 / 3628800))))
    )
    odd = (quarter == 1.0) | (quarter == 3.0)
    cos_flip = jnp.where((quarter == 1.0) | (quarter == 2.0), -1.0, 1.0)
    sin_flip = jnp.where((quarter == 2.0) | (quarter == 3.0), -1.0, 1.0)
    return cos_flip * jnp.where(odd, sine, cosine), sin_flip * jnp.where(odd, cosine, sine)


def kernel(
    sizes,
    fields_ref,
    solid_ref,
    panels_ref,
    owner_ref,
    cells_ref,
    geom_ref,
    strips_ref,
    modes_ref,
    out_ref,
    modal_ref,
    state,
    update,
    result,
    solid_in,
    owner_in,
    cells_in,
    geom_in,
    strips_in,
    modes_in,
    x_send,
    x_recv,
    x_both,
    y_send,
    y_recv,
    pan_in,
    pan_send,
    pan_recv,
    co_send,
    co_recv,
    co_rows,
    wave,
    target,
    press,
    md_send,
    md_recv,
    sd_recv,
    local_sem,
    halo_s,
    halo_r,
    pan_s,
    pan_r,
    co_s,
    co_r,
    md_s,
    md_r,
    sd_s,
    sd_r,
):
    n_stream, n_span, n_vert = sizes
    tiles = n_span * n_vert
    depth, span_cells, wind = fields_ref.shape[1:]
    half = depth // PARTS
    per_group = min(FIELDS, (wind // 2) // half)
    groups = -(-FIELDS // per_group)
    held = panels_ref.shape[1]
    spec_cols = panels_ref.shape[2]
    spec = spec_cols // 2
    strip_share = modes_ref.shape[1] // n_span
    n_modes = modes_ref.shape[2]
    deck = cells_ref.shape[3]
    me = (lax.axis_index("stream"), lax.axis_index("span"), lax.axis_index("vert"))
    stream_pos, span_pos, vert_pos = me
    my_tile = span_pos * n_vert + vert_pos

    def tile_peer(step):
        peer = lax.rem(my_tile + step, tiles)
        whole = lax.div(peer, jnp.int32(n_vert))
        return peer, (stream_pos, whole, peer - whole * n_vert)

    def stream_peer(step):
        peer = lax.rem(stream_pos + step, n_stream)
        return peer, (peer, span_pos, vert_pos)

    def any_peer(step):
        peer = lax.rem(stream_pos * tiles + my_tile + step, n_stream * tiles)
        stream = lax.div(peer, jnp.int32(tiles))
        rest = peer - stream * tiles
        whole = lax.div(rest, jnp.int32(n_vert))
        return peer, (stream, whole, rest - whole * n_vert)

    one_hop = n_stream * tiles <= ONE_HOP
    if one_hop:
        meets = [(any_peer, n_stream * tiles)]
        hops = [(any_peer, n_stream * tiles, stream_pos * tiles + my_tile)]
    else:
        meets = [(tile_peer, tiles), (stream_peer, n_stream)]
        hops = [(tile_peer, tiles, my_tile), (stream_peer, n_stream, stream_pos)]
    barrier = pltpu.get_barrier_semaphore()
    for peers, count in meets:
        for step in range(1, count):
            pl.semaphore_signal(barrier, inc=1, device_id=peers(step)[1], device_id_type=MESH)

    loads = [
        pltpu.make_async_copy(src, dst, local_sem.at[i])
        for i, (src, dst) in enumerate(
            [
                (fields_ref, state.at[:, pl.ds(1, depth)]),
                (panels_ref, pan_in),
                (owner_ref, owner_in),
                (solid_ref, solid_in),
                (cells_ref, cells_in),
                (geom_ref.at[0, span_pos], geom_in),
                (strips_ref.at[0, span_pos], strips_in),
                (modes_ref, modes_in),
            ]
        )
    ]
    for load in loads:
        load.start()

    total_z, total_y = depth * n_vert, span_cells * n_span
    period = total_y * total_z
    plane = depth * span_cells
    cell_z, cell_y = split_index(lax.broadcasted_iota(jnp.int32, (plane, spec), 0), span_cells)
    upward, across = split_index(lax.broadcasted_iota(jnp.int32, (plane, spec), 1), wave_cols)
    phase = across * (span_pos * span_cells + cell_y) * total_z
    phase = phase + upward * (vert_pos * depth + cell_z) * total_y
    phase = split_index(phase, period)[1]
    cosine, sine = circle(phase.astype(jnp.float32) * (1.0 / period))
    for i, values in enumerate((cosine, sine)):
        top = values.astype(jnp.bfloat16)
        rest = (values - top.astype(jnp.float32)).astype(jnp.bfloat16)
        wave[:, i * spec : (i + 1) * spec] = top
        wave[:, spec_cols + i * spec : spec_cols + (i + 1) * spec] = top
        wave[:, 2 * spec_cols + i * spec : 2 * spec_cols + (i + 1) * spec] = rest

    def halo(axis, way, src, dst, sem):
        count, place = sizes[axis], me[axis]
        up = way == 0
        to = lax.rem(place + (1 if up else count - 1), count)
        device = tuple(to if a == axis else me[a] for a in range(3))
        sends = place < count - 1 if up else place > 0
        gets = place > 0 if up else place < count - 1

        def copy():
            return pltpu.make_async_remote_copy(
                src_ref=src,
                dst_ref=dst,
                send_sem=halo_s.at[sem],
                recv_sem=halo_r.at[sem],
                device_id=device,
                device_id_type=MESH,
            )

        def start():
            pl.when(sends)(lambda: copy().start())

        def arrive():
            pl.when(gets)(lambda: copy().wait_recv())

        def leave():
            pl.when(sends)(lambda: copy().wait_send())

        def clear():
            @pl.when(jnp.logical_not(gets))
            def _():
                dst[...] = jnp.zeros(dst.shape, jnp.float32)

        return start, arrive, leave, clear

    z_first = [
        halo(2, 0, fields_ref.at[:, depth - 1], state.at[:, 0], 0),
        halo(2, 1, fields_ref.at[:, 0], state.at[:, depth + 1], 1),
    ]
    z_second = [
        halo(2, 0, update.at[:, depth], update.at[:, 0], 2),
        halo(2, 1, update.at[:, 1], update.at[:, depth + 1], 3),
    ]
    xy_first, xy_second = (
        [
            [
                halo(
                    1,
                    way,
                    y_send.at[stage, way, part],
                    y_recv.at[stage, way, part],
                    4 + 8 * stage + 4 * part + way,
                )
                for way in range(2)
            ]
            + [
                halo(
                    0,
                    way,
                    x_send.at[stage, part],
                    x_recv.at[stage, way, part],
                    6 + 8 * stage + 4 * part + way,
                )
                for way in range(2)
            ]
            for part in range(PARTS)
        ]
        for stage in range(2)
    )
    every_halo = z_first + z_second + sum(xy_first + xy_second, [])

    lane = lax.broadcasted_iota(jnp.int32, (span_cells, wind), 1)
    row = lax.broadcasted_iota(jnp.int32, (span_cells, wind), 0)
    lane_pair = lane >> 1

    def pack(stage, part, z, values, held_x):
        packed = list(held_x)
        for f in range(FIELDS):
            y_send[stage, 0, part, f, pl.ds(z, 1), :] = values[f][span_cells - 1 : span_cells, :]
            y_send[stage, 1, part, f, pl.ds(z, 1), :] = values[f][0:1, :]
            pair = (f % per_group) * half + z
            turned = pltpu.roll(values[f], 2 * pair + 1, 1)
            g = f // per_group
            packed[g] = jnp.where(lane_pair == pair, turned, packed[g])
        return tuple(packed)

    no_columns = tuple(jnp.zeros((span_cells, wind), jnp.float32) for _ in range(groups))

    def spread(peers, count, src, dst, mine, send_sem, recv_sem):
        copies = []
        for step in range(1, count):
            peer, device = peers(step)
            copy = pltpu.make_async_remote_copy(
                src_ref=src(peer),
                dst_ref=dst.at[mine],
                send_sem=send_sem.at[peer],
                recv_sem=recv_sem.at[mine],
                device_id=device,
                device_id_type=MESH,
            )
            copy.start()
            arrival = pltpu.make_async_remote_copy(
                src_ref=src(peer),
                dst_ref=dst.at[peer],
                send_sem=send_sem.at[peer],
                recv_sem=recv_sem.at[peer],
                device_id=device,
                device_id_type=MESH,
            )
            copies.append((copy, arrival))
        return copies

    loads[0].wait()
    for part in range(PARTS):

        def pack_plane(z, held_x, part=part):
            values = [state[f, 1 + part * half + z] for f in range(FIELDS)]
            return pack(0, part, z, values, held_x)

        packed = lax.fori_loop(0, half, pack_plane, no_columns, unroll=4)
        for g in range(groups):
            x_send[0, part, g] = packed[g]
        if part == 0:
            pl.semaphore_wait(barrier, sum(count - 1 for _, count in meets))
        for start, _, _, _ in xy_first[part] + [z_first[part]]:
            start()
    for _, _, _, clear in every_halo:
        clear()

    loads[1].wait()
    loads[2].wait()
    owner = jnp.broadcast_to(owner_in[...], (tiles, held))
    wanted_by = lax.broadcasted_iota(jnp.int32, (tiles, held), 0)
    route = jnp.where(owner == wanted_by, 1.0, 0.0)
    for f in range(FIELDS):
        sums = jnp.dot(
            route, pan_in[f], precision=HIGHEST, preferred_element_type=jnp.float32
        )
        for t in range(tiles):
            pan_send[t, :, f * spec_cols : (f + 1) * spec_cols] = sums[t : t + 1, :]

    pan_copies = spread(
        tile_peer, tiles, lambda peer: pan_send.at[peer], pan_recv, my_tile, pan_s, pan_r
    )
    pan_recv[my_tile] = pan_send[my_tile]

    even = (lane & 1) == 0

    def columns(stage, part):
        for g in range(groups):
            from_low = pltpu.roll(x_recv[stage, 0, part, g], 1, 1)
            from_high = pltpu.roll(x_recv[stage, 1, part, g], wind - 1, 1)
            x_both[stage, part, g] = jnp.where(even, from_high, from_low)

    spots = stream_pos * wind + lane
    relax = jnp.where(
        spots < wind // 2, jnp.exp(spots.astype(jnp.float32) * (-1.0 / relax_depth)) / relax_time, 0.0
    )
    relax_dt = time_step * relax
    diffusion = [viscous] * 4 + [heat_diff]
    keep = {nu: 1.0 - time_step * (6.0 * nu) - relax_dt for nu in set(diffusion)}
    half_dt = 0.5 * time_step

    every_field = tuple(range(FIELDS))

    def inflow_term(at, only):
        wanted = target[pl.ds(pl.multiple_of(at * span_cells, span_cells), span_cells), :]
        return {
            f: relax_dt * jnp.broadcast_to(wanted[:, f : f + 1], (span_cells, wind))
            for f in only
        }

    def advance(source, stage, part, z, inflow=True, only=every_field):
        at = part * half + z
        terms = inflow_term(at, only) if inflow else None
        centre = [source[f, 1 + at] for f in range(FIELDS)]
        u, v, w = (half_dt * centre[f] for f in range(3))
        sides = {}

        def x_sides(f):
            if ("x", f) not in sides:
                c = centre[f]
                pair = (f % per_group) * half + z
                side = pltpu.roll(x_both[stage, part, f // per_group], wind - 1 - 2 * pair, 1)
                west = jnp.where(lane == 0, side, pltpu.roll(c, 1, 1))
                east = jnp.where(lane == wind - 1, side, pltpu.roll(c, wind - 1, 1))
                sides["x", f] = east - west, east + west
            return sides["x", f]

        def y_sides(f):
            if ("y", f) not in sides:
                c = centre[f]
                low = jnp.broadcast_to(y_recv[stage, 0, part, f, pl.ds(z, 1), :], c.shape)
                high = jnp.broadcast_to(y_recv[stage, 1, part, f, pl.ds(z, 1), :], c.shape)
                south = jnp.where(row == 0, low, pltpu.roll(c, 1, 0))
                north = jnp.where(row == span_cells - 1, high, pltpu.roll(c, span_cells - 1, 0))
                sides["y", f] = north - south, north + south
            return sides["y", f]

        def z_sides(f):
            if ("z", f) not in sides:
                lower, upper = source[f, at], source[f, at + 2]
                sides["z", f] = upper - lower, upper + lower
            return sides["z", f]

        damping = (2.0 / penalty) * solid_in[at] if only != (3,) else None
        new = {}
        for f in only:
            (dx, sum_x), (dy, sum_y), (dz, sum_z) = x_sides(f), y_sides(f), z_sides(f)
            nu = diffusion[f]
            value = keep[nu] * centre[f] + (time_step * nu) * (sum_x + sum_y + sum_z)
            if inflow:
                value = value + terms[f]
            new[f] = value - (u * dx + v * dy + w * dz)
        for f, sided, speed in ((0, x_sides, u), (1, y_sides, v), (2, z_sides, w)):
            if f in new:
                new[f] = new[f] - half_dt * sided(3)[0] - damping * speed
        if 2 in new:
            new[2] = new[2] + (time_step * buoyant) * centre[4]
        if 3 in new:
            spread_out = x_sides(0)[0] + y_sides(1)[0] + z_sides(2)[0]
            new[3] = new[3] - (half_dt * sound_sq) * spread_out
        return new

    loads[3].wait()
    for _, arrive, _, _ in xy_first[0] + [z_first[0]]:
        arrive()
    columns(0, 0)

    def plain_plane(z, carry):
        new = advance(state, 0, 0, z, inflow=False)
        for f in range(FIELDS):
            update[f, 1 + z] = new[f]
        return carry

    lax.fori_loop(0, half // 2, plain_plane, 0, unroll=4)

    for _, arrival in pan_copies:
        arrival.wait_recv()
    mine = pan_recv[0]
    for t in range(1, tiles):
        mine = mine + pan_recv[t]
    co_send[...] = mine
    co_copies = spread(
        stream_peer, n_stream, lambda peer: co_send, co_recv, stream_pos, co_s, co_r
    )
    co_recv[stream_pos] = mine

    lax.fori_loop(half // 2, half, plain_plane, 0, unroll=4)

    for _, arrival in co_copies:
        arrival.wait_recv()
    coeffs = co_recv[0]
    for t in range(1, n_stream):
        coeffs = coeffs + co_recv[t]
    co_rows[...] = jnp.zeros_like(co_rows)
    for f in range(FIELDS):
        co_rows[f : f + 1, :] = coeffs[:, f * spec_cols : (f + 1) * spec_cols]
    top = co_rows[...].astype(jnp.bfloat16)
    rest = (co_rows[...] - top.astype(jnp.float32)).astype(jnp.bfloat16)
    inflow = lax.dot_general(
        wave[...],
        jnp.concatenate([top, rest, top], axis=1),
        (((1,), (1,)), ((), ())),
        preferred_element_type=jnp.float32,
    )
    first_field = lax.broadcasted_iota(jnp.int32, inflow.shape, 1) == 0
    target[...] = inflow + jnp.where(first_field, 1.0, 0.0)

    def finish_plane(z, held_x):
        terms = inflow_term(z, every_field)
        new = [update[f, 1 + z] + terms[f] for f in range(FIELDS)]
        for f in range(FIELDS):
            update[f, 1 + z] = new[f]
        return pack(1, 0, z, new, held_x)

    def first_plane(z, held_x):
        new = advance(state, 0, 1, z)
        for f in range(FIELDS):
            update[f, 1 + half + z] = new[f]
        return pack(1, 1, z, new, held_x)

    for part, step_plane in enumerate((finish_plane, first_plane)):
        if part == 1:
            for _, arrive, _, _ in xy_first[1] + [z_first[1]]:
                arrive()
            columns(0, 1)
        packed = lax.fori_loop(0, half, step_plane, no_columns, unroll=4)
        for g in range(groups):
            x_send[1, part, g] = packed[g]
        for start, _, _, _ in xy_second[part]:
            start()
        z_second[1 - part][0]()

    def second_plane(part, z, only=every_field):
        new = advance(update, 1, part, z, only=only)
        at = part * half + z
        for f in only:
            value = 0.5 * (state[f, 1 + at] + new[f])
            result[f, at] = value
            if f == 3:
                top = value.astype(jnp.bfloat16)
                rest = (value - top.astype(jnp.float32)).astype(jnp.bfloat16)
                where = pl.ds(pl.multiple_of(at * span_cells, span_cells), span_cells)
                press[where, 0:wind] = top
                press[where, wind:] = rest

    def store(part):
        where = pl.ds(part * half, half)
        return pltpu.make_async_copy(
            result.at[:, where], out_ref.at[:, where], local_sem.at[8 + part]
        )

    for part in range(PARTS):
        for _, arrive, _, _ in xy_second[part]:
            arrive()
        columns(1, part)
        if part == PARTS - 1:
            z_second[1][1]()

        def plane_step(z, carry, part=part):
            second_plane(part, z, every_field if part == 0 else (3,))
            return carry

        if part == 0:
            lax.fori_loop(half // 4, half, plane_step, 0, unroll=4)
            z_second[0][1]()
            lax.fori_loop(0, half // 4, plane_step, 0, unroll=4)
            store(0).start()
        else:
            lax.fori_loop(0, half, plane_step, 0, unroll=4)

    for load in loads[4:]:
        load.wait()
    width = min(deck, 256)
    base = span_pos * strip_share
    hit_row = lax.broadcasted_iota(jnp.int32, (plane, width), 0)
    hit_col = lax.broadcasted_iota(jnp.int32, (wind, width), 0)

    def deck_step(i, totals):
        where = pl.ds(pl.multiple_of(i * width, width), width)
        cell_row, cell_col = split_index(cells_in[0, 0, :, where], wind)
        pick = jnp.where(hit_col == cell_col, 1.0, 0.0).astype(jnp.bfloat16)
        pick = jnp.concatenate([pick, pick], axis=0)
        rows = jnp.dot(press[...], pick, preferred_element_type=jnp.float32)
        sampled = jnp.sum(jnp.where(hit_row == cell_row, rows, 0.0), axis=0, keepdims=True)
        traction = [sampled * geom_in[c, :, where] for c in range(3)]
        strip = strips_in[:, where]
        return tuple(
            total + jnp.where(strip == base + n // 3, traction[n % 3], 0.0)
            for n, total in enumerate(totals)
        )

    totals = lax.fori_loop(
        0,
        deck // width,
        deck_step,
        tuple(jnp.zeros((1, width), jnp.float32) for _ in range(3 * strip_share)),
        unroll=2,
    )
    force = jnp.sum(jnp.concatenate(totals, axis=0), axis=1, keepdims=True)
    shapes = jnp.concatenate(
        [modes_in[n % 3, pl.ds(base + n // 3, 1), :] for n in range(3 * strip_share)], axis=0
    )
    part_force = jnp.sum(force * shapes, axis=0, keepdims=True)

    def other_fields(z, carry):
        second_plane(1, z, (0, 1, 2, 4))
        return carry

    md_copies = []
    slots = ((md_recv, md_s, md_r), (sd_recv, sd_s, sd_r))
    for hop, (peers, count, mine) in enumerate(hops):
        recv, send_sem, recv_sem = slots[hop]
        md_send[hop] = jnp.zeros(md_send.shape[1:], jnp.float32)
        md_send[hop, :, 0:n_modes] = part_force
        copies = spread(
            peers, count, lambda peer, hop=hop: md_send.at[hop], recv, mine, send_sem, recv_sem
        )
        recv[mine] = md_send[hop]
        if hop == 0:
            lax.fori_loop(0, half, other_fields, 0, unroll=4)
            store(1).start()
            for copy, _ in pan_copies + co_copies:
                copy.wait_send()
            for _, _, leave, _ in every_halo:
                leave()
            for part in range(PARTS):
                store(part).wait()
        for _, arrival in copies:
            arrival.wait_recv()
        total = recv[0]
        for t in range(1, count):
            total = total + recv[t]
        part_force = total[:, 0:n_modes]
        md_copies = md_copies + copies
    modal_ref[...] = part_force
    for copy, _ in md_copies:
        copy.wait_send()


def place(fields_ref, modal_ref, out_ref, force_ref, sem):
    count = fields_ref.shape[0]
    pieces = [(modal_ref, force_ref)]
    pieces += [(fields_ref.at[f], out_ref.at[f]) for f in range(count)]
    copies = [
        pltpu.make_async_copy(src, dst, sem.at[i]) for i, (src, dst) in enumerate(pieces)
    ]
    for copy in copies:
        copy.start()
    for copy in copies:
        copy.wait()


def on_device(sizes, fields, solid, panels, owner, cells, geom, strips, modes):
    n_stream, n_span, n_vert = sizes
    tiles = n_span * n_vert
    depth, span_cells, wind = fields.shape[1:]
    half = depth // PARTS
    per_group = min(FIELDS, (wind // 2) // half)
    groups = -(-FIELDS // per_group)
    spec_cols = panels.shape[2]
    n_modes = modes.shape[2]
    plane = depth * span_cells
    f32 = jnp.float32
    dma = pltpu.SemaphoreType.DMA
    vmem = pl.BlockSpec(memory_space=pltpu.VMEM)
    hbm = pl.BlockSpec(memory_space=pltpu.HBM)
    held = panels.shape[0]
    if n_stream * tiles <= ONE_HOP:
        first_hop, second_hop = n_stream * tiles, 1
    else:
        first_hop, second_hop = tiles, n_stream
    panels = panels.transpose(1, 0, 2)
    owner = owner.reshape(1, held)
    geom = geom.transpose(0, 1, 3, 2, 4)
    new_fields, modal = pl.pallas_call(
        functools.partial(kernel, sizes),
        out_shape=(
            jax.ShapeDtypeStruct(fields.shape, f32),
            jax.ShapeDtypeStruct((1, n_modes), f32),
        ),
        in_specs=[hbm] * 8,
        out_specs=(hbm, vmem),
        scratch_shapes=[
            pltpu.VMEM((FIELDS, depth + 2, span_cells, wind), f32),
            pltpu.VMEM((FIELDS, depth + 2, span_cells, wind), f32),
            pltpu.VMEM((FIELDS, depth, span_cells, wind), f32),
            pltpu.VMEM(solid.shape, f32),
            pltpu.VMEM(owner.shape, jnp.int32),
            pltpu.VMEM(cells.shape, jnp.int32),
            pltpu.VMEM(geom.shape[2:], f32),
            pltpu.VMEM(strips.shape[2:], jnp.int32),
            pltpu.VMEM(modes.shape, f32),
            pltpu.VMEM((2, PARTS, groups, span_cells, wind), f32),
            pltpu.VMEM((2, 2, PARTS, groups, span_cells, wind), f32),
            pltpu.VMEM((2, PARTS, groups, span_cells, wind), f32),
            pltpu.VMEM((2, 2, PARTS, FIELDS, half, wind), f32),
            pltpu.VMEM((2, 2, PARTS, FIELDS, half, wind), f32),
            pltpu.VMEM(panels.shape, f32),
            pltpu.VMEM((tiles, 1, FIELDS * spec_cols), f32),
            pltpu.VMEM((tiles, 1, FIELDS * spec_cols), f32),
            pltpu.VMEM((1, FIELDS * spec_cols), f32),
            pltpu.VMEM((n_stream, 1, FIELDS * spec_cols), f32),
            pltpu.VMEM((16, spec_cols), f32),
            pltpu.VMEM((plane, 3 * spec_cols), jnp.bfloat16),
            pltpu.VMEM((plane, 16), f32),
            pltpu.VMEM((plane, 2 * wind), jnp.bfloat16),
            pltpu.VMEM((2, 1, 128), f32),
            pltpu.VMEM((first_hop, 1, 128), f32),
            pltpu.VMEM((second_hop, 1, 128), f32),
            dma((8 + PARTS,)),
            dma((4 + 8 * PARTS,)),
            dma((4 + 8 * PARTS,)),
            dma((tiles,)),
            dma((tiles,)),
            dma((n_stream,)),
            dma((n_stream,)),
            dma((first_hop,)),
            dma((first_hop,)),
            dma((second_hop,)),
            dma((second_hop,)),
        ],
        compiler_params=pltpu.CompilerParams(
            collective_id=0, has_side_effects=True, vmem_limit_bytes=63 * 1024 * 1024
        ),
        name="wind_steps",
    )(fields, solid, panels, owner, cells, geom, strips, modes)
    new_fields, modal = pl.pallas_call(
        place,
        out_shape=(
            jax.ShapeDtypeStruct(fields.shape, f32),
            jax.ShapeDtypeStruct((1, n_modes), f32),
        ),
        in_specs=[hbm, hbm],
        out_specs=(hbm, hbm),
        scratch_shapes=[
            dma((FIELDS + 1,)),
        ],
        compiler_params=pltpu.CompilerParams(vmem_limit_bytes=63 * 1024 * 1024),
        name="place_results",
    )(new_fields, modal)
    return new_fields, modal[0]


def solution(mesh):
    sizes = tuple(mesh.shape[axis] for axis in ("stream", "span", "vert"))
    return jax.shard_map(
        functools.partial(on_device, sizes),
        mesh=mesh,
        in_specs=(
            P(None, "vert", "span", "stream"),
            P("vert", "span", "stream"),
            P(("stream", "span", "vert"), None, None),
            P(("stream", "span", "vert"), None),
            P("vert", "span", "stream", None),
            P("vert", None, "stream", None, None),
            P("vert", None, "stream", None),
            P(),
        ),
        out_specs=(P(None, "vert", "span", "stream"), P()),
        check_vma=False,
    )
```

```python
import functools
import itertools
import math

import jax
import jax.numpy as jnp
from jax import lax
from jax.experimental import pallas as pl
from jax.experimental.pallas import tpu as pltpu
from jax.sharding import PartitionSpec as P

MESH = pl.DeviceIdType.MESH
HIGHEST = lax.Precision.HIGHEST

time_step = 0.15
viscous = 0.05
heat_diff = 0.03
sound_sq = 1.0
buoyant = 0.5
penalty = 0.5
relax_time = 0.5
relax_depth = 8.0
wave_cols = 16
FIELDS = 5
PARTS = 2
ONE_HOP = 64


def split_index(values, size):
    if size & (size - 1) == 0:
        return values >> (size.bit_length() - 1), values & (size - 1)
    whole = lax.div(values, jnp.int32(size))
    return whole, values - whole * size


def circle(turns):
    quarter = jnp.floor(4.0 * turns + 0.5)
    angle = (turns - 0.25 * quarter) * (2.0 * math.pi)
    sq = angle * angle
    sine = angle * (
        1.0 + sq * (-1.0 / 6 + sq * (1.0 / 120 + sq * (-1.0 / 5040 + sq * (1.0 / 362880))))
    )
    cosine = 1.0 + sq * (
        -0.5 + sq * (1.0 / 24 + sq * (-1.0 / 720 + sq * (1.0 / 40320 + sq * (-1.0 / 3628800))))
    )
    odd = (quarter == 1.0) | (quarter == 3.0)
    cos_flip = jnp.where((quarter == 1.0) | (quarter == 2.0), -1.0, 1.0)
    sin_flip = jnp.where((quarter == 2.0) | (quarter == 3.0), -1.0, 1.0)
    return cos_flip * jnp.where(odd, sine, cosine), sin_flip * jnp.where(odd, cosine, sine)


def kernel(
    sizes,
    fields_ref,
    solid_ref,
    panels_ref,
    owner_ref,
    cells_ref,
    geom_ref,
    strips_ref,
    modes_ref,
    out_ref,
    modal_ref,
    state,
    update,
    result,
    solid_in,
    owner_in,
    cells_in,
    geom_in,
    strips_in,
    modes_in,
    x_send,
    x_recv,
    x_both,
    y_send,
    y_recv,
    pan_in,
    pan_send,
    pan_recv,
    co_send,
    co_recv,
    co_rows,
    wave,
    target,
    press,
    md_send,
    md_recv,
    sd_recv,
    local_sem,
    halo_s,
    halo_r,
    pan_s,
    pan_r,
    co_s,
    co_r,
    md_s,
    md_r,
    sd_s,
    sd_r,
):
    n_stream, n_span, n_vert = sizes
    tiles = n_span * n_vert
    depth, span_cells, wind = fields_ref.shape[1:]
    half = depth // PARTS
    per_group = min(FIELDS, (wind // 2) // half)
    groups = -(-FIELDS // per_group)
    held = panels_ref.shape[1]
    spec_cols = panels_ref.shape[2]
    spec = spec_cols // 2
    strip_share = modes_ref.shape[1] // n_span
    n_modes = modes_ref.shape[2]
    deck = cells_ref.shape[3]
    me = (lax.axis_index("stream"), lax.axis_index("span"), lax.axis_index("vert"))
    stream_pos, span_pos, vert_pos = me
    my_tile = span_pos * n_vert + vert_pos

    def wrapped(place, offset, count):
        moved = place + offset
        return jnp.where(moved >= count, moved - count, moved)

    def peers_over(axes):
        found = []
        for offsets in itertools.product(*(range(sizes[a]) for a in axes)):
            if any(offsets):
                device, slot = list(me), 0
                for a, offset in zip(axes, offsets):
                    device[a] = wrapped(me[a], offset, sizes[a]) if offset else me[a]
                    slot = slot * sizes[a] + device[a]
                found.append((slot, tuple(device)))
        return found

    tile_peers = peers_over((1, 2))
    stream_peers = peers_over((0,))
    if n_stream * tiles <= ONE_HOP:
        all_peers = peers_over((0, 1, 2))
        meets = all_peers
        hops = [(all_peers, stream_pos * tiles + my_tile)]
    else:
        meets = tile_peers + stream_peers
        hops = [(tile_peers, my_tile), (stream_peers, stream_pos)]
    barrier = pltpu.get_barrier_semaphore()
    for _, device in meets:
        pl.semaphore_signal(barrier, inc=1, device_id=device, device_id_type=MESH)

    loads = [
        pltpu.make_async_copy(src, dst, local_sem.at[i])
        for i, (src, dst) in enumerate(
            [
                (fields_ref, state.at[:, pl.ds(1, depth)]),
                (panels_ref, pan_in),
                (owner_ref, owner_in),
                (solid_ref, solid_in),
                (cells_ref, cells_in),
                (geom_ref.at[0, span_pos], geom_in),
                (strips_ref.at[0, span_pos], strips_in),
                (modes_ref, modes_in),
            ]
        )
    ]
    for load in loads:
        load.start()

    total_z, total_y = depth * n_vert, span_cells * n_span
    period = total_y * total_z
    plane = depth * span_cells
    cell_z, cell_y = split_index(lax.broadcasted_iota(jnp.int32, (plane, spec), 0), span_cells)
    upward, across = split_index(lax.broadcasted_iota(jnp.int32, (plane, spec), 1), wave_cols)
    phase = across * (span_pos * span_cells + cell_y) * total_z
    phase = phase + upward * (vert_pos * depth + cell_z) * total_y
    phase = split_index(phase, period)[1]
    cosine, sine = circle(phase.astype(jnp.float32) * (1.0 / period))
    for i, values in enumerate((cosine, sine)):
        top = values.astype(jnp.bfloat16)
        rest = (values - top.astype(jnp.float32)).astype(jnp.bfloat16)
        wave[:, i * spec : (i + 1) * spec] = top
        wave[:, spec_cols + i * spec : spec_cols + (i + 1) * spec] = top
        wave[:, 2 * spec_cols + i * spec : 2 * spec_cols + (i + 1) * spec] = rest

    def halo(axis, way, src, dst, sem):
        count, place = sizes[axis], me[axis]
        up = way == 0
        to = wrapped(place, 1 if up else count - 1, count)
        device = tuple(to if a == axis else me[a] for a in range(3))
        sends = place < count - 1 if up else place > 0
        gets = place > 0 if up else place < count - 1

        def copy():
            return pltpu.make_async_remote_copy(
                src_ref=src,
                dst_ref=dst,
                send_sem=halo_s.at[sem],
                recv_sem=halo_r.at[sem],
                device_id=device,
                device_id_type=MESH,
            )

        def start():
            pl.when(sends)(lambda: copy().start())

        def arrive():
            pl.when(gets)(lambda: copy().wait_recv())

        def leave():
            pl.when(sends)(lambda: copy().wait_send())

        def clear():
            @pl.when(jnp.logical_not(gets))
            def _():
                dst[...] = jnp.zeros(dst.shape, jnp.float32)

        return start, arrive, leave, clear

    z_first = [
        halo(2, 0, state.at[:, depth], state.at[:, 0], 0),
        halo(2, 1, state.at[:, 1], state.at[:, depth + 1], 1),
    ]
    z_second = [
        halo(2, 0, update.at[:, depth], update.at[:, 0], 2),
        halo(2, 1, update.at[:, 1], update.at[:, depth + 1], 3),
    ]
    xy_first, xy_second = (
        [
            [
                halo(
                    1,
                    way,
                    y_send.at[stage, way, part],
                    y_recv.at[stage, way, part],
                    4 + 8 * stage + 4 * part + way,
                )
                for way in range(2)
            ]
            + [
                halo(
                    0,
                    way,
                    x_send.at[stage, part],
                    x_recv.at[stage, way, part],
                    6 + 8 * stage + 4 * part + way,
                )
                for way in range(2)
            ]
            for part in range(PARTS)
        ]
        for stage in range(2)
    )
    every_halo = z_first + z_second + sum(xy_first + xy_second, [])

    lane = lax.broadcasted_iota(jnp.int32, (span_cells, wind), 1)
    row = lax.broadcasted_iota(jnp.int32, (span_cells, wind), 0)
    lane_pair = lane >> 1

    def pack(stage, part, z, values, held_x):
        packed = list(held_x)
        for f in range(FIELDS):
            y_send[stage, 0, part, f, pl.ds(z, 1), :] = values[f][span_cells - 1 : span_cells, :]
            y_send[stage, 1, part, f, pl.ds(z, 1), :] = values[f][0:1, :]
            pair = (f % per_group) * half + z
            turned = pltpu.roll(values[f], 2 * pair + 1, 1)
            g = f // per_group
            packed[g] = jnp.where(lane_pair == pair, turned, packed[g])
        return tuple(packed)

    no_columns = tuple(jnp.zeros((span_cells, wind), jnp.float32) for _ in range(groups))

    def spread(peers, src, dst, mine, send_sem, recv_sem):
        for slot, device in peers:
            pltpu.make_async_remote_copy(
                src_ref=src(slot),
                dst_ref=dst.at[mine],
                send_sem=send_sem.at[0],
                recv_sem=recv_sem.at[0],
                device_id=device,
                device_id_type=MESH,
            ).start()
        others = dst.at[pl.ds(0, len(peers))]

        def arrive():
            pltpu.make_async_copy(others, others, recv_sem.at[0]).wait()

        def leave():
            pltpu.make_async_copy(others, others, send_sem.at[0]).wait()

        return arrive, leave

    loads[0].wait()
    for part in range(PARTS):

        def pack_plane(z, held_x, part=part):
            values = [state[f, 1 + part * half + z] for f in range(FIELDS)]
            return pack(0, part, z, values, held_x)

        packed = lax.fori_loop(0, half, pack_plane, no_columns, unroll=4)
        for g in range(groups):
            x_send[0, part, g] = packed[g]
        if part == 0:
            pl.semaphore_wait(barrier, len(meets))
        for start, _, _, _ in xy_first[part] + [z_first[part]]:
            start()
    for _, _, _, clear in every_halo:
        clear()

    loads[1].wait()
    loads[2].wait()
    owner = jnp.broadcast_to(owner_in[...], (tiles, held))
    wanted_by = lax.broadcasted_iota(jnp.int32, (tiles, held), 0)
    route = jnp.where(owner == wanted_by, 1.0, 0.0)
    for f in range(FIELDS):
        sums = jnp.dot(
            route, pan_in[f], precision=HIGHEST, preferred_element_type=jnp.float32
        )
        for t in range(tiles):
            pan_send[t, :, f * spec_cols : (f + 1) * spec_cols] = sums[t : t + 1, :]

    pan_arrive, pan_leave = spread(
        tile_peers, lambda slot: pan_send.at[slot], pan_recv, my_tile, pan_s, pan_r
    )
    pan_recv[my_tile] = pan_send[my_tile]

    even = (lane & 1) == 0

    def columns(stage, part):
        for g in range(groups):
            from_low = pltpu.roll(x_recv[stage, 0, part, g], 1, 1)
            from_high = pltpu.roll(x_recv[stage, 1, part, g], wind - 1, 1)
            x_both[stage, part, g] = jnp.where(even, from_high, from_low)

    spots = stream_pos * wind + lane
    relax = jnp.where(
        spots < wind // 2, jnp.exp(spots.astype(jnp.float32) * (-1.0 / relax_depth)) / relax_time, 0.0
    )
    relax_dt = time_step * relax
    diffusion = [viscous] * 4 + [heat_diff]
    keep = {nu: 1.0 - time_step * (6.0 * nu) - relax_dt for nu in set(diffusion)}
    half_dt = 0.5 * time_step

    every_field = tuple(range(FIELDS))

    def inflow_term(at, only):
        wanted = target[pl.ds(pl.multiple_of(at * span_cells, span_cells), span_cells), :]
        return {
            f: relax_dt * jnp.broadcast_to(wanted[:, f : f + 1], (span_cells, wind))
            for f in only
        }

    def advance(source, stage, part, z, inflow=True, only=every_field):
        at = part * half + z
        terms = inflow_term(at, only) if inflow else None
        centre = [source[f, 1 + at] for f in range(FIELDS)]
        u, v, w = (half_dt * centre[f] for f in range(3))
        sides = {}

        def x_sides(f):
            if ("x", f) not in sides:
                c = centre[f]
                pair = (f % per_group) * half + z
                side = pltpu.roll(x_both[stage, part, f // per_group], wind - 1 - 2 * pair, 1)
                west = jnp.where(lane == 0, side, pltpu.roll(c, 1, 1))
                east = jnp.where(lane == wind - 1, side, pltpu.roll(c, wind - 1, 1))
                sides["x", f] = east - west, east + west
            return sides["x", f]

        def y_sides(f):
            if ("y", f) not in sides:
                c = centre[f]
                low = jnp.broadcast_to(y_recv[stage, 0, part, f, pl.ds(z, 1), :], c.shape)
                high = jnp.broadcast_to(y_recv[stage, 1, part, f, pl.ds(z, 1), :], c.shape)
                south = jnp.where(row == 0, low, pltpu.roll(c, 1, 0))
                north = jnp.where(row == span_cells - 1, high, pltpu.roll(c, span_cells - 1, 0))
                sides["y", f] = north - south, north + south
            return sides["y", f]

        def z_sides(f):
            if ("z", f) not in sides:
                lower, upper = source[f, at], source[f, at + 2]
                sides["z", f] = upper - lower, upper + lower
            return sides["z", f]

        damping = (2.0 / penalty) * solid_in[at] if only != (3,) else None
        new = {}
        for f in only:
            (dx, sum_x), (dy, sum_y), (dz, sum_z) = x_sides(f), y_sides(f), z_sides(f)
            nu = diffusion[f]
            value = keep[nu] * centre[f] + (time_step * nu) * (sum_x + sum_y + sum_z)
            if inflow:
                value = value + terms[f]
            new[f] = value - (u * dx + v * dy + w * dz)
        for f, sided, speed in ((0, x_sides, u), (1, y_sides, v), (2, z_sides, w)):
            if f in new:
                new[f] = new[f] - half_dt * sided(3)[0] - damping * speed
        if 2 in new:
            new[2] = new[2] + (time_step * buoyant) * centre[4]
        if 3 in new:
            spread_out = x_sides(0)[0] + y_sides(1)[0] + z_sides(2)[0]
            new[3] = new[3] - (half_dt * sound_sq) * spread_out
        return new

    loads[3].wait()
    for _, arrive, _, _ in xy_first[0] + [z_first[0]]:
        arrive()
    columns(0, 0)

    def plain_plane(z, carry):
        new = advance(state, 0, 0, z, inflow=False)
        for f in range(FIELDS):
            update[f, 1 + z] = new[f]
        return carry

    lax.fori_loop(0, half // 2, plain_plane, 0, unroll=4)

    pan_arrive()
    mine = pan_recv[0]
    for t in range(1, tiles):
        mine = mine + pan_recv[t]
    co_send[...] = mine
    co_arrive, co_leave = spread(
        stream_peers, lambda slot: co_send, co_recv, stream_pos, co_s, co_r
    )
    co_recv[stream_pos] = mine

    lax.fori_loop(half // 2, half, plain_plane, 0, unroll=4)

    co_arrive()
    coeffs = co_recv[0]
    for t in range(1, n_stream):
        coeffs = coeffs + co_recv[t]
    co_rows[...] = jnp.zeros_like(co_rows)
    for f in range(FIELDS):
        co_rows[f : f + 1, :] = coeffs[:, f * spec_cols : (f + 1) * spec_cols]
    top = co_rows[...].astype(jnp.bfloat16)
    rest = (co_rows[...] - top.astype(jnp.float32)).astype(jnp.bfloat16)
    inflow = lax.dot_general(
        wave[...],
        jnp.concatenate([top, rest, top], axis=1),
        (((1,), (1,)), ((), ())),
        preferred_element_type=jnp.float32,
    )
    first_field = lax.broadcasted_iota(jnp.int32, inflow.shape, 1) == 0
    target[...] = inflow + jnp.where(first_field, 1.0, 0.0)

    def finish_plane(z, held_x):
        terms = inflow_term(z, every_field)
        new = [update[f, 1 + z] + terms[f] for f in range(FIELDS)]
        for f in range(FIELDS):
            update[f, 1 + z] = new[f]
        return pack(1, 0, z, new, held_x)

    def first_plane(z, held_x):
        new = advance(state, 0, 1, z)
        for f in range(FIELDS):
            update[f, 1 + half + z] = new[f]
        return pack(1, 1, z, new, held_x)

    for part, step_plane in enumerate((finish_plane, first_plane)):
        if part == 1:
            for _, arrive, _, _ in xy_first[1] + [z_first[1]]:
                arrive()
            columns(0, 1)
        packed = lax.fori_loop(0, half, step_plane, no_columns, unroll=4)
        for g in range(groups):
            x_send[1, part, g] = packed[g]
        for start, _, _, _ in xy_second[part]:
            start()
        z_second[1 - part][0]()

    def second_plane(part, z, only=every_field):
        new = advance(update, 1, part, z, only=only)
        at = part * half + z
        for f in only:
            value = 0.5 * (state[f, 1 + at] + new[f])
            result[f, at] = value
            if f == 3:
                top = value.astype(jnp.bfloat16)
                rest = (value - top.astype(jnp.float32)).astype(jnp.bfloat16)
                where = pl.ds(pl.multiple_of(at * span_cells, span_cells), span_cells)
                press[where, 0:wind] = top
                press[where, wind:] = rest

    def store(part):
        where = pl.ds(part * half, half)
        return pltpu.make_async_copy(
            result.at[:, where], out_ref.at[:, where], local_sem.at[8 + part]
        )

    for part in range(PARTS):
        for _, arrive, _, _ in xy_second[part]:
            arrive()
        columns(1, part)
        if part == PARTS - 1:
            z_second[1][1]()

        def plane_step(z, carry, part=part):
            second_plane(part, z, every_field if part == 0 else (3,))
            return carry

        if part == 0:
            lax.fori_loop(half // 4, half, plane_step, 0, unroll=4)
            z_second[0][1]()
            lax.fori_loop(0, half // 4, plane_step, 0, unroll=4)
            store(0).start()
        else:
            lax.fori_loop(0, half, plane_step, 0, unroll=4)

    for load in loads[4:]:
        load.wait()
    width = min(deck, 256)
    base = span_pos * strip_share
    hit_row = lax.broadcasted_iota(jnp.int32, (plane, width), 0)
    hit_col = lax.broadcasted_iota(jnp.int32, (wind, width), 0)

    def deck_step(i, totals):
        where = pl.ds(pl.multiple_of(i * width, width), width)
        cell_row, cell_col = split_index(cells_in[0, 0, :, where], wind)
        pick = jnp.where(hit_col == cell_col, 1.0, 0.0).astype(jnp.bfloat16)
        pick = jnp.concatenate([pick, pick], axis=0)
        rows = jnp.dot(press[...], pick, preferred_element_type=jnp.float32)
        sampled = jnp.sum(jnp.where(hit_row == cell_row, rows, 0.0), axis=0, keepdims=True)
        traction = [sampled * geom_in[c, :, where] for c in range(3)]
        strip = strips_in[:, where]
        return tuple(
            total + jnp.where(strip == base + n // 3, traction[n % 3], 0.0)
            for n, total in enumerate(totals)
        )

    totals = lax.fori_loop(
        0,
        deck // width,
        deck_step,
        tuple(jnp.zeros((1, width), jnp.float32) for _ in range(3 * strip_share)),
        unroll=2,
    )
    force = jnp.sum(jnp.concatenate(totals, axis=0), axis=1, keepdims=True)
    shapes = jnp.concatenate(
        [modes_in[n % 3, pl.ds(base + n // 3, 1), :] for n in range(3 * strip_share)], axis=0
    )
    part_force = jnp.sum(force * shapes, axis=0, keepdims=True)

    def other_fields(z, carry):
        second_plane(1, z, (0, 1, 2, 4))
        return carry

    leaves = [pan_leave, co_leave] + [leave for _, _, leave, _ in every_halo]
    slots = ((md_recv, md_s, md_r), (sd_recv, sd_s, sd_r))
    for hop, (peers, mine) in enumerate(hops):
        recv, send_sem, recv_sem = slots[hop]
        md_send[hop] = jnp.zeros(md_send.shape[1:], jnp.float32)
        md_send[hop, :, 0:n_modes] = part_force
        arrive, leave = spread(
            peers, lambda slot, hop=hop: md_send.at[hop], recv, mine, send_sem, recv_sem
        )
        recv[mine] = md_send[hop]
        if hop == 0:
            lax.fori_loop(0, half, other_fields, 0, unroll=4)
            store(1).start()
            for done in leaves:
                done()
            for part in range(PARTS):
                store(part).wait()
        arrive()
        total = recv[0]
        for t in range(1, len(peers) + 1):
            total = total + recv[t]
        part_force = total[:, 0:n_modes]
        leave()
    modal_ref[...] = part_force


def place(fields_ref, modal_ref, out_ref, force_ref, held, force, in_sem, out_sem):
    count = fields_ref.shape[0]
    pieces = [(fields_ref.at[f], held.at[f], out_ref.at[f]) for f in range(count)]
    pieces += [(modal_ref, force, force_ref)]
    comes = [
        pltpu.make_async_copy(src, mid, in_sem.at[i]) for i, (src, mid, _) in enumerate(pieces)
    ]
    goes = [
        pltpu.make_async_copy(mid, dst, out_sem.at[i]) for i, (_, mid, dst) in enumerate(pieces)
    ]
    for come in comes:
        come.start()
    for come, go in zip(comes, goes):
        come.wait()
        go.start()
    for go in goes:
        go.wait()


def on_device(sizes, fields, solid, panels, owner, cells, geom, strips, modes):
    n_stream, n_span, n_vert = sizes
    tiles = n_span * n_vert
    depth, span_cells, wind = fields.shape[1:]
    half = depth // PARTS
    per_group = min(FIELDS, (wind // 2) // half)
    groups = -(-FIELDS // per_group)
    spec_cols = panels.shape[2]
    n_modes = modes.shape[2]
    plane = depth * span_cells
    f32 = jnp.float32
    dma = pltpu.SemaphoreType.DMA
    vmem = pl.BlockSpec(memory_space=pltpu.VMEM)
    hbm = pl.BlockSpec(memory_space=pltpu.HBM)
    held = panels.shape[0]
    if n_stream * tiles <= ONE_HOP:
        first_hop, second_hop = n_stream * tiles, 1
    else:
        first_hop, second_hop = tiles, n_stream
    panels = panels.transpose(1, 0, 2)
    owner = owner.reshape(1, held)
    geom = geom.transpose(0, 1, 3, 2, 4)
    new_fields, modal = pl.pallas_call(
        functools.partial(kernel, sizes),
        out_shape=(
            jax.ShapeDtypeStruct(fields.shape, f32),
            jax.ShapeDtypeStruct((1, n_modes), f32),
        ),
        in_specs=[hbm] * 8,
        out_specs=(hbm, vmem),
        scratch_shapes=[
            pltpu.VMEM((FIELDS, depth + 2, span_cells, wind), f32),
            pltpu.VMEM((FIELDS, depth + 2, span_cells, wind), f32),
            pltpu.VMEM((FIELDS, depth, span_cells, wind), f32),
            pltpu.VMEM(solid.shape, f32),
            pltpu.VMEM(owner.shape, jnp.int32),
            pltpu.VMEM(cells.shape, jnp.int32),
            pltpu.VMEM(geom.shape[2:], f32),
            pltpu.VMEM(strips.shape[2:], jnp.int32),
            pltpu.VMEM(modes.shape, f32),
            pltpu.VMEM((2, PARTS, groups, span_cells, wind), f32),
            pltpu.VMEM((2, 2, PARTS, groups, span_cells, wind), f32),
            pltpu.VMEM((2, PARTS, groups, span_cells, wind), f32),
            pltpu.VMEM((2, 2, PARTS, FIELDS, half, wind), f32),
            pltpu.VMEM((2, 2, PARTS, FIELDS, half, wind), f32),
            pltpu.VMEM(panels.shape, f32),
            pltpu.VMEM((tiles, 1, FIELDS * spec_cols), f32),
            pltpu.VMEM((tiles, 1, FIELDS * spec_cols), f32),
            pltpu.VMEM((1, FIELDS * spec_cols), f32),
            pltpu.VMEM((n_stream, 1, FIELDS * spec_cols), f32),
            pltpu.VMEM((16, spec_cols), f32),
            pltpu.VMEM((plane, 3 * spec_cols), jnp.bfloat16),
            pltpu.VMEM((plane, 16), f32),
            pltpu.VMEM((plane, 2 * wind), jnp.bfloat16),
            pltpu.VMEM((2, 1, 128), f32),
            pltpu.VMEM((first_hop, 1, 128), f32),
            pltpu.VMEM((second_hop, 1, 128), f32),
            dma((8 + PARTS,)),
            dma((4 + 8 * PARTS,)),
            dma((4 + 8 * PARTS,)),
            dma((1,)),
            dma((1,)),
            dma((1,)),
            dma((1,)),
            dma((1,)),
            dma((1,)),
            dma((1,)),
            dma((1,)),
        ],
        compiler_params=pltpu.CompilerParams(
            collective_id=0, has_side_effects=True, vmem_limit_bytes=63 * 1024 * 1024
        ),
        name="wind_steps",
    )(fields, solid, panels, owner, cells, geom, strips, modes)
    new_fields, modal = pl.pallas_call(
        place,
        out_shape=(
            jax.ShapeDtypeStruct(fields.shape, f32),
            jax.ShapeDtypeStruct((1, n_modes), f32),
        ),
        in_specs=[hbm, hbm],
        out_specs=(hbm, hbm),
        scratch_shapes=[
            pltpu.VMEM(fields.shape, f32),
            pltpu.VMEM((1, n_modes), f32),
            dma((FIELDS + 1,)),
            dma((FIELDS + 1,)),
        ],
        compiler_params=pltpu.CompilerParams(vmem_limit_bytes=63 * 1024 * 1024),
        name="place_results",
    )(new_fields, modal)
    return new_fields, modal[0]


def solution(mesh):
    sizes = tuple(mesh.shape[axis] for axis in ("stream", "span", "vert"))
    return jax.shard_map(
        functools.partial(on_device, sizes),
        mesh=mesh,
        in_specs=(
            P(None, "vert", "span", "stream"),
            P("vert", "span", "stream"),
            P(("stream", "span", "vert"), None, None),
            P(("stream", "span", "vert"), None),
            P("vert", "span", "stream", None),
            P("vert", None, "stream", None, None),
            P("vert", None, "stream", None),
            P(),
        ),
        out_specs=(P(None, "vert", "span", "stream"), P()),
        check_vma=False,
    )
```

```python
import functools
import itertools
import math

import jax
import jax.numpy as jnp
from jax import lax
from jax.experimental import pallas as pl
from jax.experimental.pallas import tpu as pltpu
from jax.sharding import PartitionSpec as P

MESH = pl.DeviceIdType.MESH
HIGHEST = lax.Precision.HIGHEST

time_step = 0.15
viscous = 0.05
heat_diff = 0.03
sound_sq = 1.0
buoyant = 0.5
penalty = 0.5
relax_time = 0.5
relax_depth = 8.0
wave_cols = 16
FIELDS = 5
PARTS = 2
ONE_HOP = 64


def split_index(values, size):
    if size & (size - 1) == 0:
        return values >> (size.bit_length() - 1), values & (size - 1)
    whole = lax.div(values, jnp.int32(size))
    return whole, values - whole * size


def circle(turns):
    quarter = jnp.floor(4.0 * turns + 0.5)
    angle = (turns - 0.25 * quarter) * (2.0 * math.pi)
    sq = angle * angle
    sine = angle * (
        1.0 + sq * (-1.0 / 6 + sq * (1.0 / 120 + sq * (-1.0 / 5040 + sq * (1.0 / 362880))))
    )
    cosine = 1.0 + sq * (
        -0.5 + sq * (1.0 / 24 + sq * (-1.0 / 720 + sq * (1.0 / 40320 + sq * (-1.0 / 3628800))))
    )
    odd = (quarter == 1.0) | (quarter == 3.0)
    cos_flip = jnp.where((quarter == 1.0) | (quarter == 2.0), -1.0, 1.0)
    sin_flip = jnp.where((quarter == 2.0) | (quarter == 3.0), -1.0, 1.0)
    return cos_flip * jnp.where(odd, sine, cosine), sin_flip * jnp.where(odd, cosine, sine)


def kernel(
    sizes,
    fields_ref,
    solid_ref,
    panels_ref,
    owner_ref,
    cells_ref,
    geom_ref,
    strips_ref,
    modes_ref,
    out_ref,
    modal_ref,
    state,
    update,
    result,
    solid_in,
    owner_in,
    cells_in,
    geom_in,
    strips_in,
    modes_in,
    x_send,
    x_recv,
    x_both,
    y_send,
    y_recv,
    pan_in,
    pan_send,
    pan_recv,
    co_send,
    co_recv,
    co_rows,
    wave,
    target,
    nudge,
    press,
    md_send,
    md_recv,
    sd_recv,
    local_sem,
    halo_s,
    halo_r,
    pan_s,
    pan_r,
    co_s,
    co_r,
    md_s,
    md_r,
    sd_s,
    sd_r,
):
    n_stream, n_span, n_vert = sizes
    tiles = n_span * n_vert
    depth, span_cells, wind = fields_ref.shape[1:]
    half = depth // PARTS
    per_group = min(FIELDS, (wind // 2) // half)
    groups = -(-FIELDS // per_group)
    held = panels_ref.shape[1]
    spec_cols = panels_ref.shape[2]
    spec = spec_cols // 2
    strip_share = modes_ref.shape[1] // n_span
    n_modes = modes_ref.shape[2]
    deck = cells_ref.shape[3]
    me = (lax.axis_index("stream"), lax.axis_index("span"), lax.axis_index("vert"))
    stream_pos, span_pos, vert_pos = me
    my_tile = span_pos * n_vert + vert_pos

    def wrapped(place, offset, count):
        moved = place + offset
        return jnp.where(moved >= count, moved - count, moved)

    def peers_over(axes):
        found = []
        for offsets in itertools.product(*(range(sizes[a]) for a in axes)):
            if any(offsets):
                device, slot = list(me), 0
                for a, offset in zip(axes, offsets):
                    device[a] = wrapped(me[a], offset, sizes[a]) if offset else me[a]
                    slot = slot * sizes[a] + device[a]
                found.append((slot, tuple(device)))
        return found

    tile_peers = peers_over((1, 2))
    stream_peers = peers_over((0,))
    if n_stream * tiles <= ONE_HOP:
        all_peers = peers_over((0, 1, 2))
        meets = all_peers
        hops = [(all_peers, stream_pos * tiles + my_tile)]
    else:
        meets = tile_peers + stream_peers
        hops = [(tile_peers, my_tile), (stream_peers, stream_pos)]
    barrier = pltpu.get_barrier_semaphore()
    for _, device in meets:
        pl.semaphore_signal(barrier, inc=1, device_id=device, device_id_type=MESH)

    loads = [
        pltpu.make_async_copy(src, dst, local_sem.at[i])
        for i, (src, dst) in enumerate(
            [
                (fields_ref, state.at[:, pl.ds(1, depth)]),
                (panels_ref, pan_in),
                (owner_ref, owner_in),
                (solid_ref, solid_in),
                (cells_ref, cells_in),
                (geom_ref.at[0, span_pos], geom_in),
                (strips_ref.at[0, span_pos], strips_in),
                (modes_ref, modes_in),
            ]
        )
    ]
    for load in loads:
        load.start()

    total_z, total_y = depth * n_vert, span_cells * n_span
    period = total_y * total_z
    plane = depth * span_cells
    cell_z, cell_y = split_index(lax.broadcasted_iota(jnp.int32, (plane, spec), 0), span_cells)
    upward, across = split_index(lax.broadcasted_iota(jnp.int32, (plane, spec), 1), wave_cols)
    phase = across * (span_pos * span_cells + cell_y) * total_z
    phase = phase + upward * (vert_pos * depth + cell_z) * total_y
    phase = split_index(phase, period)[1]
    cosine, sine = circle(phase.astype(jnp.float32) * (1.0 / period))
    for i, values in enumerate((cosine, sine)):
        top = values.astype(jnp.bfloat16)
        rest = (values - top.astype(jnp.float32)).astype(jnp.bfloat16)
        wave[:, i * spec : (i + 1) * spec] = top
        wave[:, spec_cols + i * spec : spec_cols + (i + 1) * spec] = top
        wave[:, 2 * spec_cols + i * spec : 2 * spec_cols + (i + 1) * spec] = rest

    def halo(axis, way, src, dst, sem):
        count, place = sizes[axis], me[axis]
        up = way == 0
        to = wrapped(place, 1 if up else count - 1, count)
        device = tuple(to if a == axis else me[a] for a in range(3))
        sends = place < count - 1 if up else place > 0
        gets = place > 0 if up else place < count - 1

        def copy():
            return pltpu.make_async_remote_copy(
                src_ref=src,
                dst_ref=dst,
                send_sem=halo_s.at[sem],
                recv_sem=halo_r.at[sem],
                device_id=device,
                device_id_type=MESH,
            )

        def start():
            pl.when(sends)(lambda: copy().start())

        def arrive():
            pl.when(gets)(lambda: copy().wait_recv())

        def leave():
            pl.when(sends)(lambda: copy().wait_send())

        def clear():
            @pl.when(jnp.logical_not(gets))
            def _():
                dst[...] = jnp.zeros(dst.shape, jnp.float32)

        return start, arrive, leave, clear

    z_first = [
        halo(2, 0, state.at[:, depth], state.at[:, 0], 0),
        halo(2, 1, state.at[:, 1], state.at[:, depth + 1], 1),
    ]
    z_second = [
        halo(2, 0, update.at[:, depth], update.at[:, 0], 2),
        halo(2, 1, update.at[:, 1], update.at[:, depth + 1], 3),
    ]
    xy_first, xy_second = (
        [
            [
                halo(
                    1,
                    way,
                    y_send.at[stage, way, part],
                    y_recv.at[stage, way, part],
                    4 + 8 * stage + 4 * part + way,
                )
                for way in range(2)
            ]
            + [
                halo(
                    0,
                    way,
                    x_send.at[stage, part],
                    x_recv.at[stage, way, part],
                    6 + 8 * stage + 4 * part + way,
                )
                for way in range(2)
            ]
            for part in range(PARTS)
        ]
        for stage in range(2)
    )
    every_halo = z_first + z_second + sum(xy_first + xy_second, [])

    lane = lax.broadcasted_iota(jnp.int32, (span_cells, wind), 1)
    row = lax.broadcasted_iota(jnp.int32, (span_cells, wind), 0)
    lane_pair = lane >> 1

    def pack(stage, part, z, values, held_x):
        packed = list(held_x)
        for f in range(FIELDS):
            y_send[stage, 0, part, f, pl.ds(z, 1), :] = values[f][span_cells - 1 : span_cells, :]
            y_send[stage, 1, part, f, pl.ds(z, 1), :] = values[f][0:1, :]
            pair = (f % per_group) * half + z
            turned = pltpu.roll(values[f], 2 * pair + 1, 1)
            g = f // per_group
            packed[g] = jnp.where(lane_pair == pair, turned, packed[g])
        return tuple(packed)

    no_columns = tuple(jnp.zeros((span_cells, wind), jnp.float32) for _ in range(groups))

    def spread(peers, src, dst, mine, send_sem, recv_sem):
        for slot, device in peers:
            pltpu.make_async_remote_copy(
                src_ref=src(slot),
                dst_ref=dst.at[mine],
                send_sem=send_sem.at[0],
                recv_sem=recv_sem.at[0],
                device_id=device,
                device_id_type=MESH,
            ).start()
        others = dst.at[pl.ds(0, len(peers))]

        def arrive():
            pltpu.make_async_copy(others, others, recv_sem.at[0]).wait()

        def leave():
            pltpu.make_async_copy(others, others, send_sem.at[0]).wait()

        return arrive, leave

    loads[0].wait()
    for part in range(PARTS):

        def pack_plane(z, held_x, part=part):
            values = [state[f, 1 + part * half + z] for f in range(FIELDS)]
            return pack(0, part, z, values, held_x)

        packed = lax.fori_loop(0, half, pack_plane, no_columns, unroll=4)
        for g in range(groups):
            x_send[0, part, g] = packed[g]
        if part == 0:
            pl.semaphore_wait(barrier, len(meets))
        for start, _, _, _ in xy_first[part] + [z_first[part]]:
            start()
    for _, _, _, clear in every_halo:
        clear()

    loads[1].wait()
    loads[2].wait()
    owner = jnp.broadcast_to(owner_in[...], (tiles, held))
    wanted_by = lax.broadcasted_iota(jnp.int32, (tiles, held), 0)
    route = jnp.where(owner == wanted_by, 1.0, 0.0)
    for f in range(FIELDS):
        sums = jnp.dot(
            route, pan_in[f], precision=HIGHEST, preferred_element_type=jnp.float32
        )
        for t in range(tiles):
            pan_send[t, :, f * spec_cols : (f + 1) * spec_cols] = sums[t : t + 1, :]

    pan_arrive, pan_leave = spread(
        tile_peers, lambda slot: pan_send.at[slot], pan_recv, my_tile, pan_s, pan_r
    )
    pan_recv[my_tile] = pan_send[my_tile]

    even = (lane & 1) == 0

    def columns(stage, part):
        for g in range(groups):
            from_low = pltpu.roll(x_recv[stage, 0, part, g], 1, 1)
            from_high = pltpu.roll(x_recv[stage, 1, part, g], wind - 1, 1)
            x_both[stage, part, g] = jnp.where(even, from_high, from_low)

    spots = stream_pos * wind + lane
    relax = jnp.where(
        spots < wind // 2, jnp.exp(spots.astype(jnp.float32) * (-1.0 / relax_depth)) / relax_time, 0.0
    )
    relax_dt = time_step * relax
    diffusion = [viscous] * 4 + [heat_diff]
    keep = {nu: 1.0 - time_step * (6.0 * nu) - relax_dt for nu in set(diffusion)}
    half_dt = 0.5 * time_step

    every_field = tuple(range(FIELDS))

    def inflow_term(at, only):
        wanted = target[pl.ds(pl.multiple_of(at * span_cells, span_cells), span_cells), :]
        terms = {
            f: relax_dt * jnp.broadcast_to(wanted[:, f : f + 1], (span_cells, wind))
            for f in only
        }
        for f in only:
            nudge[f, at] = terms[f]
        return terms

    def advance(source, stage, part, z, inflow=True, only=every_field):
        at = part * half + z
        if inflow:
            terms = inflow_term(at, only) if stage == 0 else {f: nudge[f, at] for f in only}
        centre = [source[f, 1 + at] for f in range(FIELDS)]
        u, v, w = (half_dt * centre[f] for f in range(3))
        sides = {}

        def x_sides(f):
            if ("x", f) not in sides:
                c = centre[f]
                pair = (f % per_group) * half + z
                side = pltpu.roll(x_both[stage, part, f // per_group], wind - 1 - 2 * pair, 1)
                west = jnp.where(lane == 0, side, pltpu.roll(c, 1, 1))
                east = jnp.where(lane == wind - 1, side, pltpu.roll(c, wind - 1, 1))
                sides["x", f] = east - west, east + west
            return sides["x", f]

        def y_sides(f):
            if ("y", f) not in sides:
                c = centre[f]
                low = jnp.broadcast_to(y_recv[stage, 0, part, f, pl.ds(z, 1), :], c.shape)
                high = jnp.broadcast_to(y_recv[stage, 1, part, f, pl.ds(z, 1), :], c.shape)
                south = jnp.where(row == 0, low, pltpu.roll(c, 1, 0))
                north = jnp.where(row == span_cells - 1, high, pltpu.roll(c, span_cells - 1, 0))
                sides["y", f] = north - south, north + south
            return sides["y", f]

        def z_sides(f):
            if ("z", f) not in sides:
                lower, upper = source[f, at], source[f, at + 2]
                sides["z", f] = upper - lower, upper + lower
            return sides["z", f]

        damping = (2.0 / penalty) * solid_in[at] if only != (3,) else None
        new = {}
        for f in only:
            (dx, sum_x), (dy, sum_y), (dz, sum_z) = x_sides(f), y_sides(f), z_sides(f)
            nu = diffusion[f]
            value = keep[nu] * centre[f] + (time_step * nu) * (sum_x + sum_y + sum_z)
            if inflow:
                value = value + terms[f]
            new[f] = value - (u * dx + v * dy + w * dz)
        for f, sided, speed in ((0, x_sides, u), (1, y_sides, v), (2, z_sides, w)):
            if f in new:
                new[f] = new[f] - half_dt * sided(3)[0] - damping * speed
        if 2 in new:
            new[2] = new[2] + (time_step * buoyant) * centre[4]
        if 3 in new:
            spread_out = x_sides(0)[0] + y_sides(1)[0] + z_sides(2)[0]
            new[3] = new[3] - (half_dt * sound_sq) * spread_out
        return new

    loads[3].wait()
    for _, arrive, _, _ in xy_first[0] + [z_first[0]]:
        arrive()
    columns(0, 0)

    def plain_plane(z, carry):
        new = advance(state, 0, 0, z, inflow=False)
        for f in range(FIELDS):
            update[f, 1 + z] = new[f]
        return carry

    lax.fori_loop(0, half // 2, plain_plane, 0, unroll=4)

    pan_arrive()
    mine = pan_recv[0]
    for t in range(1, tiles):
        mine = mine + pan_recv[t]
    co_send[...] = mine
    co_arrive, co_leave = spread(
        stream_peers, lambda slot: co_send, co_recv, stream_pos, co_s, co_r
    )
    co_recv[stream_pos] = mine

    lax.fori_loop(half // 2, half, plain_plane, 0, unroll=4)

    co_arrive()
    coeffs = co_recv[0]
    for t in range(1, n_stream):
        coeffs = coeffs + co_recv[t]
    co_rows[...] = jnp.zeros_like(co_rows)
    for f in range(FIELDS):
        co_rows[f : f + 1, :] = coeffs[:, f * spec_cols : (f + 1) * spec_cols]
    top = co_rows[...].astype(jnp.bfloat16)
    rest = (co_rows[...] - top.astype(jnp.float32)).astype(jnp.bfloat16)
    inflow = lax.dot_general(
        wave[...],
        jnp.concatenate([top, rest, top], axis=1),
        (((1,), (1,)), ((), ())),
        preferred_element_type=jnp.float32,
    )
    first_field = lax.broadcasted_iota(jnp.int32, inflow.shape, 1) == 0
    target[...] = inflow + jnp.where(first_field, 1.0, 0.0)

    def finish_plane(z, held_x):
        terms = inflow_term(z, every_field)
        new = [update[f, 1 + z] + terms[f] for f in range(FIELDS)]
        for f in range(FIELDS):
            update[f, 1 + z] = new[f]
        return pack(1, 0, z, new, held_x)

    def first_plane(z, held_x):
        new = advance(state, 0, 1, z)
        for f in range(FIELDS):
            update[f, 1 + half + z] = new[f]
        return pack(1, 1, z, new, held_x)

    for part, step_plane in enumerate((finish_plane, first_plane)):
        if part == 1:
            for _, arrive, _, _ in xy_first[1] + [z_first[1]]:
                arrive()
            columns(0, 1)
        packed = lax.fori_loop(0, half, step_plane, no_columns, unroll=4)
        for g in range(groups):
            x_send[1, part, g] = packed[g]
        for start, _, _, _ in xy_second[part]:
            start()
        z_second[1 - part][0]()

    def second_plane(part, z, only=every_field):
        new = advance(update, 1, part, z, only=only)
        at = part * half + z
        for f in only:
            value = 0.5 * (state[f, 1 + at] + new[f])
            result[f, at] = value
            if f == 3:
                top = value.astype(jnp.bfloat16)
                rest = (value - top.astype(jnp.float32)).astype(jnp.bfloat16)
                where = pl.ds(pl.multiple_of(at * span_cells, span_cells), span_cells)
                press[where, 0:wind] = top
                press[where, wind:] = rest

    def store(part):
        where = pl.ds(part * half, half)
        return pltpu.make_async_copy(
            result.at[:, where], out_ref.at[:, where], local_sem.at[8 + part]
        )

    for part in range(PARTS):
        for _, arrive, _, _ in xy_second[part]:
            arrive()
        columns(1, part)
        if part == PARTS - 1:
            z_second[1][1]()

        def plane_step(z, carry, part=part):
            second_plane(part, z, every_field if part == 0 else (3,))
            return carry

        if part == 0:
            lax.fori_loop(half // 4, half, plane_step, 0, unroll=4)
            z_second[0][1]()
            lax.fori_loop(0, half // 4, plane_step, 0, unroll=4)
            store(0).start()
        else:
            lax.fori_loop(0, half, plane_step, 0, unroll=4)

    for load in loads[4:]:
        load.wait()
    width = min(deck, 256)
    base = span_pos * strip_share
    hit_row = lax.broadcasted_iota(jnp.int32, (plane, width), 0)
    hit_col = lax.broadcasted_iota(jnp.int32, (wind, width), 0)

    def deck_step(i, totals):
        where = pl.ds(pl.multiple_of(i * width, width), width)
        cell_row, cell_col = split_index(cells_in[0, 0, :, where], wind)
        pick = jnp.where(hit_col == cell_col, 1.0, 0.0).astype(jnp.bfloat16)
        pick = jnp.concatenate([pick, pick], axis=0)
        rows = jnp.dot(press[...], pick, preferred_element_type=jnp.float32)
        sampled = jnp.sum(jnp.where(hit_row == cell_row, rows, 0.0), axis=0, keepdims=True)
        traction = [sampled * geom_in[c, :, where] for c in range(3)]
        strip = strips_in[:, where]
        return tuple(
            total + jnp.where(strip == base + n // 3, traction[n % 3], 0.0)
            for n, total in enumerate(totals)
        )

    totals = lax.fori_loop(
        0,
        deck // width,
        deck_step,
        tuple(jnp.zeros((1, width), jnp.float32) for _ in range(3 * strip_share)),
        unroll=2,
    )
    force = jnp.sum(jnp.concatenate(totals, axis=0), axis=1, keepdims=True)
    shapes = jnp.concatenate(
        [modes_in[n % 3, pl.ds(base + n // 3, 1), :] for n in range(3 * strip_share)], axis=0
    )
    part_force = jnp.sum(force * shapes, axis=0, keepdims=True)

    def other_fields(z, carry):
        second_plane(1, z, (0, 1, 2, 4))
        return carry

    leaves = [pan_leave, co_leave] + [leave for _, _, leave, _ in every_halo]
    slots = ((md_recv, md_s, md_r), (sd_recv, sd_s, sd_r))
    for hop, (peers, mine) in enumerate(hops):
        recv, send_sem, recv_sem = slots[hop]
        md_send[hop] = jnp.zeros(md_send.shape[1:], jnp.float32)
        md_send[hop, :, 0:n_modes] = part_force
        arrive, leave = spread(
            peers, lambda slot, hop=hop: md_send.at[hop], recv, mine, send_sem, recv_sem
        )
        recv[mine] = md_send[hop]
        if hop == 0:
            lax.fori_loop(0, half, other_fields, 0, unroll=4)
            store(1).start()
            for done in leaves:
                done()
            for part in range(PARTS):
                store(part).wait()
        arrive()
        total = recv[0]
        for t in range(1, len(peers) + 1):
            total = total + recv[t]
        part_force = total[:, 0:n_modes]
        leave()
    modal_ref[...] = part_force


def place(fields_ref, modal_ref, out_ref, force_ref, held, force, in_sem, out_sem):
    count = fields_ref.shape[0]
    pieces = [(fields_ref.at[f], held.at[f], out_ref.at[f]) for f in range(count)]
    pieces += [(modal_ref, force, force_ref)]
    comes = [
        pltpu.make_async_copy(src, mid, in_sem.at[i]) for i, (src, mid, _) in enumerate(pieces)
    ]
    goes = [
        pltpu.make_async_copy(mid, dst, out_sem.at[i]) for i, (_, mid, dst) in enumerate(pieces)
    ]
    for come in comes:
        come.start()
    for come, go in zip(comes, goes):
        come.wait()
        go.start()
    for go in goes:
        go.wait()


def on_device(sizes, fields, solid, panels, owner, cells, geom, strips, modes):
    n_stream, n_span, n_vert = sizes
    tiles = n_span * n_vert
    depth, span_cells, wind = fields.shape[1:]
    half = depth // PARTS
    per_group = min(FIELDS, (wind // 2) // half)
    groups = -(-FIELDS // per_group)
    spec_cols = panels.shape[2]
    n_modes = modes.shape[2]
    plane = depth * span_cells
    f32 = jnp.float32
    dma = pltpu.SemaphoreType.DMA
    vmem = pl.BlockSpec(memory_space=pltpu.VMEM)
    hbm = pl.BlockSpec(memory_space=pltpu.HBM)
    held = panels.shape[0]
    if n_stream * tiles <= ONE_HOP:
        first_hop, second_hop = n_stream * tiles, 1
    else:
        first_hop, second_hop = tiles, n_stream
    panels = panels.transpose(1, 0, 2)
    owner = owner.reshape(1, held)
    geom = geom.transpose(0, 1, 3, 2, 4)
    new_fields, modal = pl.pallas_call(
        functools.partial(kernel, sizes),
        out_shape=(
            jax.ShapeDtypeStruct(fields.shape, f32),
            jax.ShapeDtypeStruct((1, n_modes), f32),
        ),
        in_specs=[hbm] * 8,
        out_specs=(hbm, vmem),
        scratch_shapes=[
            pltpu.VMEM((FIELDS, depth + 2, span_cells, wind), f32),
            pltpu.VMEM((FIELDS, depth + 2, span_cells, wind), f32),
            pltpu.VMEM((FIELDS, depth, span_cells, wind), f32),
            pltpu.VMEM(solid.shape, f32),
            pltpu.VMEM(owner.shape, jnp.int32),
            pltpu.VMEM(cells.shape, jnp.int32),
            pltpu.VMEM(geom.shape[2:], f32),
            pltpu.VMEM(strips.shape[2:], jnp.int32),
            pltpu.VMEM(modes.shape, f32),
            pltpu.VMEM((2, PARTS, groups, span_cells, wind), f32),
            pltpu.VMEM((2, 2, PARTS, groups, span_cells, wind), f32),
            pltpu.VMEM((2, PARTS, groups, span_cells, wind), f32),
            pltpu.VMEM((2, 2, PARTS, FIELDS, half, wind), f32),
            pltpu.VMEM((2, 2, PARTS, FIELDS, half, wind), f32),
            pltpu.VMEM(panels.shape, f32),
            pltpu.VMEM((tiles, 1, FIELDS * spec_cols), f32),
            pltpu.VMEM((tiles, 1, FIELDS * spec_cols), f32),
            pltpu.VMEM((1, FIELDS * spec_cols), f32),
            pltpu.VMEM((n_stream, 1, FIELDS * spec_cols), f32),
            pltpu.VMEM((16, spec_cols), f32),
            pltpu.VMEM((plane, 3 * spec_cols), jnp.bfloat16),
            pltpu.VMEM((plane, 16), f32),
            pltpu.VMEM((FIELDS, depth, span_cells, wind), f32),
            pltpu.VMEM((plane, 2 * wind), jnp.bfloat16),
            pltpu.VMEM((2, 1, 128), f32),
            pltpu.VMEM((first_hop, 1, 128), f32),
            pltpu.VMEM((second_hop, 1, 128), f32),
            dma((8 + PARTS,)),
            dma((4 + 8 * PARTS,)),
            dma((4 + 8 * PARTS,)),
            dma((1,)),
            dma((1,)),
            dma((1,)),
            dma((1,)),
            dma((1,)),
            dma((1,)),
            dma((1,)),
            dma((1,)),
        ],
        compiler_params=pltpu.CompilerParams(
            collective_id=0, has_side_effects=True, vmem_limit_bytes=63 * 1024 * 1024
        ),
        name="wind_steps",
    )(fields, solid, panels, owner, cells, geom, strips, modes)
    new_fields, modal = pl.pallas_call(
        place,
        out_shape=(
            jax.ShapeDtypeStruct(fields.shape, f32),
            jax.ShapeDtypeStruct((1, n_modes), f32),
        ),
        in_specs=[hbm, hbm],
        out_specs=(hbm, hbm),
        scratch_shapes=[
            pltpu.VMEM(fields.shape, f32),
            pltpu.VMEM((1, n_modes), f32),
            dma((FIELDS + 1,)),
            dma((FIELDS + 1,)),
        ],
        compiler_params=pltpu.CompilerParams(vmem_limit_bytes=63 * 1024 * 1024),
        name="place_results",
    )(new_fields, modal)
    return new_fields, modal[0]


def solution(mesh):
    sizes = tuple(mesh.shape[axis] for axis in ("stream", "span", "vert"))
    return jax.shard_map(
        functools.partial(on_device, sizes),
        mesh=mesh,
        in_specs=(
            P(None, "vert", "span", "stream"),
            P("vert", "span", "stream"),
            P(("stream", "span", "vert"), None, None),
            P(("stream", "span", "vert"), None),
            P("vert", "span", "stream", None),
            P("vert", None, "stream", None, None),
            P("vert", None, "stream", None),
            P(),
        ),
        out_specs=(P(None, "vert", "span", "stream"), P()),
        check_vma=False,
    )
```

```python
import functools
import itertools
import math

import jax
import jax.numpy as jnp
from jax import lax
from jax.experimental import pallas as pl
from jax.experimental.pallas import tpu as pltpu
from jax.sharding import PartitionSpec as P

MESH = pl.DeviceIdType.MESH
HIGHEST = lax.Precision.HIGHEST

time_step = 0.15
viscous = 0.05
heat_diff = 0.03
sound_sq = 1.0
buoyant = 0.5
penalty = 0.5
relax_time = 0.5
relax_depth = 8.0
wave_cols = 16
FIELDS = 5
PARTS = 2
ONE_HOP = 64


def split_index(values, size):
    if size & (size - 1) == 0:
        return values >> (size.bit_length() - 1), values & (size - 1)
    whole = lax.div(values, jnp.int32(size))
    return whole, values - whole * size


def circle(turns):
    quarter = jnp.floor(4.0 * turns + 0.5)
    angle = (turns - 0.25 * quarter) * (2.0 * math.pi)
    sq = angle * angle
    sine = angle * (
        1.0 + sq * (-1.0 / 6 + sq * (1.0 / 120 + sq * (-1.0 / 5040 + sq * (1.0 / 362880))))
    )
    cosine = 1.0 + sq * (
        -0.5 + sq * (1.0 / 24 + sq * (-1.0 / 720 + sq * (1.0 / 40320 + sq * (-1.0 / 3628800))))
    )
    odd = (quarter == 1.0) | (quarter == 3.0)
    cos_flip = jnp.where((quarter == 1.0) | (quarter == 2.0), -1.0, 1.0)
    sin_flip = jnp.where((quarter == 2.0) | (quarter == 3.0), -1.0, 1.0)
    return cos_flip * jnp.where(odd, sine, cosine), sin_flip * jnp.where(odd, cosine, sine)


def kernel(
    sizes,
    fields_ref,
    solid_ref,
    panels_ref,
    owner_ref,
    cells_ref,
    geom_ref,
    strips_ref,
    modes_ref,
    out_ref,
    modal_ref,
    state,
    update,
    result,
    solid_in,
    owner_in,
    cells_in,
    geom_in,
    strips_in,
    modes_in,
    x_send,
    x_recv,
    x_both,
    y_send,
    y_recv,
    pan_in,
    pan_send,
    pan_recv,
    co_send,
    co_recv,
    co_rows,
    wave,
    target,
    nudge,
    press,
    md_send,
    md_recv,
    sd_recv,
    local_sem,
    halo_s,
    halo_r,
    pan_s,
    pan_r,
    co_s,
    co_r,
    md_s,
    md_r,
    sd_s,
    sd_r,
):
    n_stream, n_span, n_vert = sizes
    tiles = n_span * n_vert
    depth, span_cells, wind = fields_ref.shape[1:]
    half = depth // PARTS
    per_group = min(FIELDS, (wind // 2) // half)
    groups = -(-FIELDS // per_group)
    held = panels_ref.shape[1]
    spec_cols = panels_ref.shape[2]
    spec = spec_cols // 2
    strip_share = modes_ref.shape[1] // n_span
    n_modes = modes_ref.shape[2]
    deck = cells_ref.shape[3]
    me = (lax.axis_index("stream"), lax.axis_index("span"), lax.axis_index("vert"))
    stream_pos, span_pos, vert_pos = me
    my_tile = span_pos * n_vert + vert_pos

    def wrapped(place, offset, count):
        moved = place + offset
        return jnp.where(moved >= count, moved - count, moved)

    def peers_over(axes):
        found = []
        for offsets in itertools.product(*(range(sizes[a]) for a in axes)):
            if any(offsets):
                device, slot = list(me), 0
                for a, offset in zip(axes, offsets):
                    device[a] = wrapped(me[a], offset, sizes[a]) if offset else me[a]
                    slot = slot * sizes[a] + device[a]
                found.append((slot, tuple(device)))
        return found

    tile_peers = peers_over((1, 2))
    stream_peers = peers_over((0,))
    if n_stream * tiles <= ONE_HOP:
        all_peers = peers_over((0, 1, 2))
        meets = all_peers
        hops = [(all_peers, stream_pos * tiles + my_tile)]
    else:
        meets = tile_peers + stream_peers
        hops = [(tile_peers, my_tile), (stream_peers, stream_pos)]
    barrier = pltpu.get_barrier_semaphore()
    for _, device in meets:
        pl.semaphore_signal(barrier, inc=1, device_id=device, device_id_type=MESH)

    loads = [
        pltpu.make_async_copy(src, dst, local_sem.at[i])
        for i, (src, dst) in enumerate(
            [
                (fields_ref, state.at[:, pl.ds(1, depth)]),
                (panels_ref, pan_in),
                (owner_ref, owner_in),
                (solid_ref, solid_in),
                (cells_ref, cells_in),
                (geom_ref.at[0, span_pos], geom_in),
                (strips_ref.at[0, span_pos], strips_in),
                (modes_ref, modes_in),
            ]
        )
    ]
    for load in loads:
        load.start()

    total_z, total_y = depth * n_vert, span_cells * n_span
    period = total_y * total_z
    plane = depth * span_cells
    cell_z, cell_y = split_index(lax.broadcasted_iota(jnp.int32, (plane, spec), 0), span_cells)
    upward, across = split_index(lax.broadcasted_iota(jnp.int32, (plane, spec), 1), wave_cols)
    phase = across * (span_pos * span_cells + cell_y) * total_z
    phase = phase + upward * (vert_pos * depth + cell_z) * total_y
    phase = split_index(phase, period)[1]
    cosine, sine = circle(phase.astype(jnp.float32) * (1.0 / period))
    for i, values in enumerate((cosine, sine)):
        top = values.astype(jnp.bfloat16)
        rest = (values - top.astype(jnp.float32)).astype(jnp.bfloat16)
        wave[:, i * spec : (i + 1) * spec] = top
        wave[:, spec_cols + i * spec : spec_cols + (i + 1) * spec] = top
        wave[:, 2 * spec_cols + i * spec : 2 * spec_cols + (i + 1) * spec] = rest

    def halo(axis, way, src, dst, sem):
        count, place = sizes[axis], me[axis]
        up = way == 0
        to = wrapped(place, 1 if up else count - 1, count)
        device = tuple(to if a == axis else me[a] for a in range(3))
        sends = place < count - 1 if up else place > 0
        gets = place > 0 if up else place < count - 1

        def copy():
            return pltpu.make_async_remote_copy(
                src_ref=src,
                dst_ref=dst,
                send_sem=halo_s.at[sem],
                recv_sem=halo_r.at[sem],
                device_id=device,
                device_id_type=MESH,
            )

        def start():
            pl.when(sends)(lambda: copy().start())

        def arrive():
            pl.when(gets)(lambda: copy().wait_recv())

        def leave():
            pl.when(sends)(lambda: copy().wait_send())

        def clear():
            @pl.when(jnp.logical_not(gets))
            def _():
                dst[...] = jnp.zeros(dst.shape, jnp.float32)

        return start, arrive, leave, clear

    z_first = [
        halo(2, 0, state.at[:, depth], state.at[:, 0], 0),
        halo(2, 1, state.at[:, 1], state.at[:, depth + 1], 1),
    ]
    z_second = [
        halo(2, 0, update.at[:, depth], update.at[:, 0], 2),
        halo(2, 1, update.at[:, 1], update.at[:, depth + 1], 3),
    ]
    xy_first, xy_second = (
        [
            [
                halo(
                    1,
                    way,
                    y_send.at[stage, way, part],
                    y_recv.at[stage, way, part],
                    4 + 8 * stage + 4 * part + way,
                )
                for way in range(2)
            ]
            + [
                halo(
                    0,
                    way,
                    x_send.at[stage, part],
                    x_recv.at[stage, way, part],
                    6 + 8 * stage + 4 * part + way,
                )
                for way in range(2)
            ]
            for part in range(PARTS)
        ]
        for stage in range(2)
    )
    every_halo = z_first + z_second + sum(xy_first + xy_second, [])

    lane = lax.broadcasted_iota(jnp.int32, (span_cells, wind), 1)
    row = lax.broadcasted_iota(jnp.int32, (span_cells, wind), 0)
    lane_pair = lane >> 1

    def pack(stage, part, z, values, held_x):
        packed = list(held_x)
        for f in range(FIELDS):
            y_send[stage, 0, part, f, pl.ds(z, 1), :] = values[f][span_cells - 1 : span_cells, :]
            y_send[stage, 1, part, f, pl.ds(z, 1), :] = values[f][0:1, :]
            pair = (f % per_group) * half + z
            turned = pltpu.roll(values[f], 2 * pair + 1, 1)
            g = f // per_group
            packed[g] = jnp.where(lane_pair == pair, turned, packed[g])
        return tuple(packed)

    no_columns = tuple(jnp.zeros((span_cells, wind), jnp.float32) for _ in range(groups))

    def spread(peers, src, dst, mine, send_sem, recv_sem):
        for slot, device in peers:
            pltpu.make_async_remote_copy(
                src_ref=src(slot),
                dst_ref=dst.at[mine],
                send_sem=send_sem.at[0],
                recv_sem=recv_sem.at[0],
                device_id=device,
                device_id_type=MESH,
            ).start()
        others = dst.at[pl.ds(0, len(peers))]

        def arrive():
            pltpu.make_async_copy(others, others, recv_sem.at[0]).wait()

        def leave():
            pltpu.make_async_copy(others, others, send_sem.at[0]).wait()

        return arrive, leave

    loads[0].wait()
    for part in range(PARTS):

        def pack_plane(z, held_x, part=part):
            values = [state[f, 1 + part * half + z] for f in range(FIELDS)]
            return pack(0, part, z, values, held_x)

        packed = lax.fori_loop(0, half, pack_plane, no_columns, unroll=4)
        for g in range(groups):
            x_send[0, part, g] = packed[g]
        if part == 0:
            pl.semaphore_wait(barrier, len(meets))
        for start, _, _, _ in xy_first[part] + [z_first[part]]:
            start()
    for _, _, _, clear in every_halo:
        clear()

    loads[1].wait()
    loads[2].wait()
    owner = jnp.broadcast_to(owner_in[...], (tiles, held))
    wanted_by = lax.broadcasted_iota(jnp.int32, (tiles, held), 0)
    route = jnp.where(owner == wanted_by, 1.0, 0.0)
    for f in range(FIELDS):
        sums = jnp.dot(
            route, pan_in[f], precision=HIGHEST, preferred_element_type=jnp.float32
        )
        for t in range(tiles):
            pan_send[t, :, f * spec_cols : (f + 1) * spec_cols] = sums[t : t + 1, :]

    pan_arrive, pan_leave = spread(
        tile_peers, lambda slot: pan_send.at[slot], pan_recv, my_tile, pan_s, pan_r
    )
    pan_recv[my_tile] = pan_send[my_tile]

    even = (lane & 1) == 0

    def columns(stage, part):
        for g in range(groups):
            from_low = pltpu.roll(x_recv[stage, 0, part, g], 1, 1)
            from_high = pltpu.roll(x_recv[stage, 1, part, g], wind - 1, 1)
            x_both[stage, part, g] = jnp.where(even, from_high, from_low)

    spots = stream_pos * wind + lane
    relax = jnp.where(
        spots < wind // 2, jnp.exp(spots.astype(jnp.float32) * (-1.0 / relax_depth)) / relax_time, 0.0
    )
    relax_dt = time_step * relax
    diffusion = [viscous] * 4 + [heat_diff]
    keep = {nu: 1.0 - time_step * (6.0 * nu) - relax_dt for nu in set(diffusion)}
    half_dt = 0.5 * time_step

    every_field = tuple(range(FIELDS))

    def inflow_term(at, only):
        wanted = target[pl.ds(pl.multiple_of(at * span_cells, span_cells), span_cells), :]
        terms = {
            f: relax_dt * jnp.broadcast_to(wanted[:, f : f + 1], (span_cells, wind))
            for f in only
        }
        for f in only:
            nudge[f, at] = terms[f]
        return terms

    def advance(source, stage, part, z, inflow=True, only=every_field):
        at = part * half + z
        if inflow:
            terms = inflow_term(at, only) if stage == 0 else {f: nudge[f, at] for f in only}
        centre = [source[f, 1 + at] for f in range(FIELDS)]
        u, v, w = (half_dt * centre[f] for f in range(3))
        sides = {}

        def x_sides(f):
            if ("x", f) not in sides:
                c = centre[f]
                pair = (f % per_group) * half + z
                side = pltpu.roll(x_both[stage, part, f // per_group], wind - 1 - 2 * pair, 1)
                west = jnp.where(lane == 0, side, pltpu.roll(c, 1, 1))
                east = jnp.where(lane == wind - 1, side, pltpu.roll(c, wind - 1, 1))
                sides["x", f] = east - west, east + west
            return sides["x", f]

        def y_sides(f):
            if ("y", f) not in sides:
                c = centre[f]
                low = jnp.broadcast_to(y_recv[stage, 0, part, f, pl.ds(z, 1), :], c.shape)
                high = jnp.broadcast_to(y_recv[stage, 1, part, f, pl.ds(z, 1), :], c.shape)
                south = jnp.where(row == 0, low, pltpu.roll(c, 1, 0))
                north = jnp.where(row == span_cells - 1, high, pltpu.roll(c, span_cells - 1, 0))
                sides["y", f] = north - south, north + south
            return sides["y", f]

        def z_sides(f):
            if ("z", f) not in sides:
                lower, upper = source[f, at], source[f, at + 2]
                sides["z", f] = upper - lower, upper + lower
            return sides["z", f]

        damping = (2.0 / penalty) * solid_in[at] if only != (3,) else None
        new = {}
        for f in only:
            (dx, sum_x), (dy, sum_y), (dz, sum_z) = x_sides(f), y_sides(f), z_sides(f)
            nu = diffusion[f]
            value = keep[nu] * centre[f] + (time_step * nu) * (sum_x + sum_y + sum_z)
            if inflow:
                value = value + terms[f]
            new[f] = value - (u * dx + v * dy + w * dz)
        for f, sided, speed in ((0, x_sides, u), (1, y_sides, v), (2, z_sides, w)):
            if f in new:
                new[f] = new[f] - half_dt * sided(3)[0] - damping * speed
        if 2 in new:
            new[2] = new[2] + (time_step * buoyant) * centre[4]
        if 3 in new:
            spread_out = x_sides(0)[0] + y_sides(1)[0] + z_sides(2)[0]
            new[3] = new[3] - (half_dt * sound_sq) * spread_out
        return new

    loads[3].wait()
    for _, arrive, _, _ in xy_first[0] + [z_first[0]]:
        arrive()
    columns(0, 0)

    def plain_plane(z, carry):
        new = advance(state, 0, 0, z, inflow=False)
        for f in range(FIELDS):
            update[f, 1 + z] = new[f]
        return carry

    lax.fori_loop(0, half // 2, plain_plane, 0, unroll=4)

    pan_arrive()
    mine = pan_recv[0]
    for t in range(1, tiles):
        mine = mine + pan_recv[t]
    co_send[...] = mine
    co_arrive, co_leave = spread(
        stream_peers, lambda slot: co_send, co_recv, stream_pos, co_s, co_r
    )
    co_recv[stream_pos] = mine

    lax.fori_loop(half // 2, half, plain_plane, 0, unroll=4)

    co_arrive()
    coeffs = co_recv[0]
    for t in range(1, n_stream):
        coeffs = coeffs + co_recv[t]
    co_rows[...] = jnp.zeros_like(co_rows)
    for f in range(FIELDS):
        co_rows[f : f + 1, :] = coeffs[:, f * spec_cols : (f + 1) * spec_cols]
    top = co_rows[...].astype(jnp.bfloat16)
    rest = (co_rows[...] - top.astype(jnp.float32)).astype(jnp.bfloat16)
    inflow = lax.dot_general(
        wave[...],
        jnp.concatenate([top, rest, top], axis=1),
        (((1,), (1,)), ((), ())),
        preferred_element_type=jnp.float32,
    )
    first_field = lax.broadcasted_iota(jnp.int32, inflow.shape, 1) == 0
    target[...] = inflow + jnp.where(first_field, 1.0, 0.0)

    def finish_plane(z, held_x):
        terms = inflow_term(z, every_field)
        new = [update[f, 1 + z] + terms[f] for f in range(FIELDS)]
        for f in range(FIELDS):
            update[f, 1 + z] = new[f]
        return pack(1, 0, z, new, held_x)

    def first_plane(z, held_x):
        new = advance(state, 0, 1, z)
        for f in range(FIELDS):
            update[f, 1 + half + z] = new[f]
        return pack(1, 1, z, new, held_x)

    for part, step_plane in enumerate((finish_plane, first_plane)):
        if part == 1:
            for _, arrive, _, _ in xy_first[1] + [z_first[1]]:
                arrive()
            columns(0, 1)
        packed = lax.fori_loop(0, half, step_plane, no_columns, unroll=4)
        for g in range(groups):
            x_send[1, part, g] = packed[g]
        for start, _, _, _ in xy_second[part]:
            start()
        z_second[1 - part][0]()

    def second_plane(part, z, only=every_field):
        new = advance(update, 1, part, z, only=only)
        at = part * half + z
        for f in only:
            value = 0.5 * (state[f, 1 + at] + new[f])
            result[f, at] = value
            if f == 3:
                top = value.astype(jnp.bfloat16)
                rest = (value - top.astype(jnp.float32)).astype(jnp.bfloat16)
                where = pl.ds(pl.multiple_of(at * span_cells, span_cells), span_cells)
                press[where, 0:wind] = top
                press[where, wind:] = rest

    def store(part):
        where = pl.ds(part * (half // 2), half // 2)
        return pltpu.make_async_copy(
            result.at[:, where], out_ref.at[:, where], local_sem.at[8 + part]
        )

    for part in range(PARTS):
        for _, arrive, _, _ in xy_second[part]:
            arrive()
        columns(1, part)
        if part == PARTS - 1:
            z_second[1][1]()

        def plane_step(z, carry, part=part):
            second_plane(part, z, every_field if part == 0 else (3,))
            return carry

        if part == 0:
            lax.fori_loop(half // 4, half, plane_step, 0, unroll=4)
            z_second[0][1]()
            lax.fori_loop(0, half // 4, plane_step, 0, unroll=4)
            store(0).start()
            store(1).start()
        else:
            lax.fori_loop(0, half, plane_step, 0, unroll=4)

    for load in loads[4:]:
        load.wait()
    width = min(deck, 256)
    base = span_pos * strip_share
    hit_row = lax.broadcasted_iota(jnp.int32, (plane, width), 0)
    hit_col = lax.broadcasted_iota(jnp.int32, (wind, width), 0)

    def deck_step(i, totals):
        where = pl.ds(pl.multiple_of(i * width, width), width)
        cell_row, cell_col = split_index(cells_in[0, 0, :, where], wind)
        pick = jnp.where(hit_col == cell_col, 1.0, 0.0).astype(jnp.bfloat16)
        pick = jnp.concatenate([pick, pick], axis=0)
        rows = jnp.dot(press[...], pick, preferred_element_type=jnp.float32)
        sampled = jnp.sum(jnp.where(hit_row == cell_row, rows, 0.0), axis=0, keepdims=True)
        traction = [sampled * geom_in[c, :, where] for c in range(3)]
        strip = strips_in[:, where]
        return tuple(
            total + jnp.where(strip == base + n // 3, traction[n % 3], 0.0)
            for n, total in enumerate(totals)
        )

    totals = lax.fori_loop(
        0,
        deck // width,
        deck_step,
        tuple(jnp.zeros((1, width), jnp.float32) for _ in range(3 * strip_share)),
        unroll=2,
    )
    force = jnp.sum(jnp.concatenate(totals, axis=0), axis=1, keepdims=True)
    shapes = jnp.concatenate(
        [modes_in[n % 3, pl.ds(base + n // 3, 1), :] for n in range(3 * strip_share)], axis=0
    )
    part_force = jnp.sum(force * shapes, axis=0, keepdims=True)

    def other_fields(z, carry):
        second_plane(1, z, (0, 1, 2, 4))
        return carry

    leaves = [pan_leave, co_leave] + [leave for _, _, leave, _ in every_halo]
    slots = ((md_recv, md_s, md_r), (sd_recv, sd_s, sd_r))
    for hop, (peers, mine) in enumerate(hops):
        recv, send_sem, recv_sem = slots[hop]
        md_send[hop] = jnp.zeros(md_send.shape[1:], jnp.float32)
        md_send[hop, :, 0:n_modes] = part_force
        arrive, leave = spread(
            peers, lambda slot, hop=hop: md_send.at[hop], recv, mine, send_sem, recv_sem
        )
        recv[mine] = md_send[hop]
        if hop == 0:
            lax.fori_loop(0, half // 2, other_fields, 0, unroll=4)
            store(2).start()
            lax.fori_loop(half // 2, half, other_fields, 0, unroll=4)
            store(3).start()
            for done in leaves:
                done()
            for part in range(2 * PARTS):
                store(part).wait()
        arrive()
        total = recv[0]
        for t in range(1, len(peers) + 1):
            total = total + recv[t]
        part_force = total[:, 0:n_modes]
        leave()
    modal_ref[...] = part_force


def place(fields_ref, modal_ref, out_ref, force_ref, held, force, in_sem, out_sem):
    count = fields_ref.shape[0]
    half = fields_ref.shape[1] // 2
    places = [(f, pl.ds(part * half, half)) for f in range(count) for part in range(2)]
    pieces = [(fields_ref.at[at], held.at[at], out_ref.at[at]) for at in places]
    pieces += [(modal_ref, force, force_ref)]
    comes = [
        pltpu.make_async_copy(src, mid, in_sem.at[i]) for i, (src, mid, _) in enumerate(pieces)
    ]
    goes = [
        pltpu.make_async_copy(mid, dst, out_sem.at[i]) for i, (_, mid, dst) in enumerate(pieces)
    ]
    for come in comes:
        come.start()
    for come, go in zip(comes, goes):
        come.wait()
        go.start()
    for go in goes:
        go.wait()


def on_device(sizes, fields, solid, panels, owner, cells, geom, strips, modes):
    n_stream, n_span, n_vert = sizes
    tiles = n_span * n_vert
    depth, span_cells, wind = fields.shape[1:]
    half = depth // PARTS
    per_group = min(FIELDS, (wind // 2) // half)
    groups = -(-FIELDS // per_group)
    spec_cols = panels.shape[2]
    n_modes = modes.shape[2]
    plane = depth * span_cells
    f32 = jnp.float32
    dma = pltpu.SemaphoreType.DMA
    vmem = pl.BlockSpec(memory_space=pltpu.VMEM)
    hbm = pl.BlockSpec(memory_space=pltpu.HBM)
    held = panels.shape[0]
    if n_stream * tiles <= ONE_HOP:
        first_hop, second_hop = n_stream * tiles, 1
    else:
        first_hop, second_hop = tiles, n_stream
    panels = panels.transpose(1, 0, 2)
    owner = owner.reshape(1, held)
    geom = geom.transpose(0, 1, 3, 2, 4)
    new_fields, modal = pl.pallas_call(
        functools.partial(kernel, sizes),
        out_shape=(
            jax.ShapeDtypeStruct(fields.shape, f32),
            jax.ShapeDtypeStruct((1, n_modes), f32),
        ),
        in_specs=[hbm] * 8,
        out_specs=(hbm, vmem),
        scratch_shapes=[
            pltpu.VMEM((FIELDS, depth + 2, span_cells, wind), f32),
            pltpu.VMEM((FIELDS, depth + 2, span_cells, wind), f32),
            pltpu.VMEM((FIELDS, depth, span_cells, wind), f32),
            pltpu.VMEM(solid.shape, f32),
            pltpu.VMEM(owner.shape, jnp.int32),
            pltpu.VMEM(cells.shape, jnp.int32),
            pltpu.VMEM(geom.shape[2:], f32),
            pltpu.VMEM(strips.shape[2:], jnp.int32),
            pltpu.VMEM(modes.shape, f32),
            pltpu.VMEM((2, PARTS, groups, span_cells, wind), f32),
            pltpu.VMEM((2, 2, PARTS, groups, span_cells, wind), f32),
            pltpu.VMEM((2, PARTS, groups, span_cells, wind), f32),
            pltpu.VMEM((2, 2, PARTS, FIELDS, half, wind), f32),
            pltpu.VMEM((2, 2, PARTS, FIELDS, half, wind), f32),
            pltpu.VMEM(panels.shape, f32),
            pltpu.VMEM((tiles, 1, FIELDS * spec_cols), f32),
            pltpu.VMEM((tiles, 1, FIELDS * spec_cols), f32),
            pltpu.VMEM((1, FIELDS * spec_cols), f32),
            pltpu.VMEM((n_stream, 1, FIELDS * spec_cols), f32),
            pltpu.VMEM((16, spec_cols), f32),
            pltpu.VMEM((plane, 3 * spec_cols), jnp.bfloat16),
            pltpu.VMEM((plane, 16), f32),
            pltpu.VMEM((FIELDS, depth, span_cells, wind), f32),
            pltpu.VMEM((plane, 2 * wind), jnp.bfloat16),
            pltpu.VMEM((2, 1, 128), f32),
            pltpu.VMEM((first_hop, 1, 128), f32),
            pltpu.VMEM((second_hop, 1, 128), f32),
            dma((8 + 2 * PARTS,)),
            dma((4 + 8 * PARTS,)),
            dma((4 + 8 * PARTS,)),
            dma((1,)),
            dma((1,)),
            dma((1,)),
            dma((1,)),
            dma((1,)),
            dma((1,)),
            dma((1,)),
            dma((1,)),
        ],
        compiler_params=pltpu.CompilerParams(
            collective_id=0, has_side_effects=True, vmem_limit_bytes=63 * 1024 * 1024
        ),
        name="wind_steps",
    )(fields, solid, panels, owner, cells, geom, strips, modes)
    new_fields, modal = pl.pallas_call(
        place,
        out_shape=(
            jax.ShapeDtypeStruct(fields.shape, f32),
            jax.ShapeDtypeStruct((1, n_modes), f32),
        ),
        in_specs=[hbm, hbm],
        out_specs=(hbm, hbm),
        scratch_shapes=[
            pltpu.VMEM(fields.shape, f32),
            pltpu.VMEM((1, n_modes), f32),
            dma((2 * FIELDS + 1,)),
            dma((2 * FIELDS + 1,)),
        ],
        compiler_params=pltpu.CompilerParams(vmem_limit_bytes=63 * 1024 * 1024),
        name="place_results",
    )(new_fields, modal)
    return new_fields, modal[0]


def solution(mesh):
    sizes = tuple(mesh.shape[axis] for axis in ("stream", "span", "vert"))
    return jax.shard_map(
        functools.partial(on_device, sizes),
        mesh=mesh,
        in_specs=(
            P(None, "vert", "span", "stream"),
            P("vert", "span", "stream"),
            P(("stream", "span", "vert"), None, None),
            P(("stream", "span", "vert"), None),
            P("vert", "span", "stream", None),
            P("vert", None, "stream", None, None),
            P("vert", None, "stream", None),
            P(),
        ),
        out_specs=(P(None, "vert", "span", "stream"), P()),
        check_vma=False,
    )
```
